256 devices in a mesh: band: 16 (over x, y), wave: 16 (over z, core).
Axes of the slice: x: 4, y: 4, z: 8, core: 2. Of those that a mesh axis runs over, the one named last changes fastest.
Arguments:
- spectral: bfloat16 [640, 1408, 8], P('wave', 'band'), may hold values from -0.119628906 to 0.119628906
- legendre: bfloat16 [640, 1280, 1408], P('wave', 'band'), may hold values from -0.15625 to 0.15625
- slot_pair: int32 [640], replicated, may hold values from 0 to 639, each once
- quad_weight: float32 [1280], P('band'), may hold values from 0.4 to 2.5
- depart_code: int32 [1, 2, 1280, 5120], P(None, None, ('band', 'wave')), may hold values from 0 to 15
- stencil_pick: int32 [1, 2, 1280, 5120], P(None, None, ('band', 'wave')), may hold values from 0 to 15
- stencil_weight: float32 [16, 16], replicated, may hold values from -0.05 to 0.175
Outputs:
- arrival: bfloat16 [1, 4, 2, 1280, 5120], P(None, None, None, ('band', 'wave'))
- spectral_out: bfloat16 [640, 1408, 8], P('wave', 'band')
The draws below stay inside these ranges and needn't reach their ends.
Inputs may be any that keep to these rules, and one draw needn't show every extreme that they name: A permutation: slot s holds the wavenumbers slot_pair[s] and 1279 - slot_pair[s]. Decodes to a latitude step depart_code // 4 - 2 and a longitude step depart_code % 4 - 2.
All inputs are finite; a program needn't handle non-finite values.
Results may differ from the reference program's by a relative error of at most 0.02.
Values may be sent and summed in bfloat16 or wider, within the bound.
A program may use at most 256 MiB of HBM per device.

```python
import math
import jax
import jax.numpy as jnp
from jax import lax

M = 1280
NLATH = 1280
NLON = 5120
FIELDS = 4
LEV = 1
DR = 2
DL = 2
NSTEN = 16
RIM = 3
COLS = 8
SLOTS = 640
NROW = 1408


def touch_ends(values, own_key, low, top_value):
    place = [jax.random.randint(jax.random.fold_in(own_key, axis), (), 0, length) for axis, length in enumerate(values.shape)]
    main_axis = values.shape.index(max(values.shape))
    next_to = place[:main_axis] + [(place[main_axis] + 1) % values.shape[main_axis]] + place[main_axis + 1:]
    return values.at[tuple(place)].set(low).at[tuple(next_to)].set(top_value)


def block_levels(stream_key, dims, cuts, low, high):
    def one(dim, blocks):
        draws = jax.random.uniform(jax.random.fold_in(jax.random.fold_in(stream_key, 6), dim), (blocks,), jnp.float32, low / len(cuts), high / len(cuts))
        return jnp.repeat(jnp.exp(draws), dims[dim] // blocks).reshape((-1,) + (1,) * (len(dims) - dim - 1))

    factor_of = one(*cuts[0])
    for cut in cuts[1:]:
        factor_of = factor_of * one(*cut)
    return factor_of


def scatter_about(rng, extent, spread, bound, split=(), held_as=jnp.bfloat16):
    loudness = block_levels(rng, extent, split, -0.22, 0.18) if split else 1.0
    entries = jax.random.normal(rng, extent, jnp.float32) * spread * loudness
    return jnp.minimum(jnp.maximum(entries, -bound), bound).astype(held_as)


def setup_inputs(seed: int = 0) -> dict:
    key_list = jax.random.split(jax.random.key(seed), 8)
    return {
        "spectral": scatter_about(key_list[0], (SLOTS, NROW, COLS), 0.02, 0.119628906, ((0, 16), (1, 16))),
        "legendre": scatter_about(key_list[1], (SLOTS, NLATH, NROW), NROW ** -0.5, 0.15625, ((0, 16), (1, 16))),
        "slot_pair": jax.random.permutation(key_list[2], SLOTS).astype(jnp.int32),
        "quad_weight": jnp.clip(jnp.exp(math.log(2.5) - 1.8325814 * jax.random.uniform(key_list[3], (NLATH,), jnp.float32) ** block_levels(key_list[3], (NLATH,), ((0, 16),), -0.2, 0.2)), 0.4, 2.5),
        "depart_code": touch_ends(jax.random.randint(key_list[4], (LEV, 2, NLATH, NLON), 0, 4 * DR * DL), jax.random.fold_in(key_list[4], 1), 0, (4 * DR * DL) - 1).astype(jnp.int32),
        "stencil_pick": touch_ends(jax.random.randint(key_list[5], (LEV, 2, NLATH, NLON), 0, NSTEN), jax.random.fold_in(key_list[5], 1), 0, NSTEN - 1).astype(jnp.int32),
        "stencil_weight": jnp.clip(jax.random.uniform(key_list[6], (NSTEN, 16), jnp.float32, -0.05, 0.175), -0.05, 0.175),
    }


def row_weights(pair_ids, row_index, wavenumbers):
    low_count = wavenumbers - pair_ids[:, None]
    higher = row_index[None, :] >= low_count
    in_use = (row_index[None, :] <= wavenumbers).astype(jnp.float32)
    degree = jnp.where(higher, row_index[None, :] - low_count, row_index[None, :])
    parity_sign = 1.0 - 2.0 * (degree % 2).astype(jnp.float32)
    high_part = higher.astype(jnp.float32)
    holder = jnp.stack([1.0 - high_part, high_part], axis=-1) * in_use[..., None]
    hemisphere = jnp.stack([jnp.ones_like(parity_sign), parity_sign], axis=-1)
    return holder[..., :, None] * hemisphere[..., None, :]

def wave_factor(slot_pair, wavenumbers):
    wave_pair = jnp.stack([slot_pair, wavenumbers - 1 - slot_pair], axis=1)
    return jnp.where(wave_pair == 0, 1.0, 2.0).astype(jnp.float32)

def angle_table(slot_pair, wavenumbers, longitudes):
    group_size = math.gcd(slot_pair.shape[0], 40)
    groups = slot_pair.reshape(-1, group_size)
    column = jnp.arange(longitudes, dtype=jnp.int32)

    def build(pair_ids):
        wave_pair = jnp.stack([pair_ids, wavenumbers - 1 - pair_ids], axis=1)
        residue = wave_pair[..., None] * column % longitudes
        angles = residue.astype(jnp.float32) * (2.0 * math.pi / longitudes)
        factor = jnp.where(wave_pair == 0, 1.0, 2.0).astype(jnp.float32)[..., None]
        result = jnp.stack([factor * jnp.cos(angles), -factor * jnp.sin(angles)], axis=2)
        return result.astype(jnp.bfloat16)
    return lax.map(build, groups).reshape(-1, longitudes)

def interpolate(padded, departure, tap_weight):
    levels, fields, hemispheres, padded_rows, longitudes = padded.shape
    height = padded_rows - 2 * RIM
    flat_values = padded.reshape(levels, fields, hemispheres * padded_rows * longitudes)
    row_shift = departure // (2 * DL) - DR
    col_shift = departure % (2 * DL) - DL
    hemi_index = jnp.arange(hemispheres, dtype=jnp.int32)[None, :, None, None]
    lat_index = jnp.arange(height, dtype=jnp.int32)[None, None, :, None]
    lon_index = jnp.arange(longitudes, dtype=jnp.int32)[None, None, None, :]
    running = jnp.zeros((levels, fields, hemispheres, height, longitudes), jnp.float32)
    for tap_index in range(16):
        source_row = lat_index + RIM + row_shift + tap_index // 4 - 1
        source_col = (lon_index + col_shift + tap_index % 4 - 1) % longitudes
        position = ((hemi_index * padded_rows + source_row) * longitudes + source_col).reshape(levels, 1, -1)
        position = jnp.broadcast_to(position, (levels, fields, position.shape[2]))
        picked = jnp.take_along_axis(flat_values, position, axis=2).reshape(running.shape)
        running = running + tap_weight(tap_index)[:, None] * picked.astype(jnp.float32)
    return running

def reference(spectral, legendre, slot_pair, quad_weight, depart_code, stencil_pick, stencil_weight):
    slot_total, row_total, col_total = spectral.shape
    group_size = math.gcd(slot_total, 40)
    masks = row_weights(slot_pair, jnp.arange(row_total, dtype=jnp.int32), M)

    def inverse_group(operands):
        spec_part, legendre_part, mask_part = operands
        masked = spec_part.astype(jnp.float32)[:, :, None, None, :] * mask_part[..., None]
        result = jnp.einsum('sjohc,sij->sohci', masked, legendre_part.astype(jnp.float32))
        return result.astype(jnp.bfloat16)
    fourier = lax.map(inverse_group, (spectral.reshape(-1, group_size, row_total, col_total), legendre.reshape(-1, group_size, NLATH, row_total), masks.reshape(-1, group_size, row_total, 2, 2)))
    fourier = fourier.reshape(slot_total, 2, 2, LEV, FIELDS, 2, NLATH)
    left_rows = fourier.transpose(3, 4, 2, 6, 0, 1, 5).reshape(LEV * FIELDS * 2 * NLATH, slot_total * 4)
    angle_rows = angle_table(slot_pair, M, NLON)
    grid_values = jnp.dot(left_rows, angle_rows, preferred_element_type=jnp.float32)
    grid_values = grid_values.astype(jnp.bfloat16).reshape(LEV, FIELDS, 2, NLATH, NLON)
    pole_rows = jnp.roll(jnp.flip(grid_values[:, :, :, :RIM], 3), NLON // 2, 4)
    equator_rows = jnp.flip(grid_values[:, :, ::-1, NLATH - RIM:], 3)
    padded = jnp.concatenate([pole_rows, grid_values, equator_rows], 3)

    def tap_weight(tap_index):
        return jnp.take(stencil_weight[:, tap_index], stencil_pick, axis=0)
    arrival = interpolate(padded, depart_code, tap_weight).astype(jnp.bfloat16)
    sums = lax.dot_general(arrival.reshape(-1, NLON), angle_rows, (((1,), (1,)), ((), ())), preferred_element_type=jnp.float32)
    sums = sums.reshape(LEV, FIELDS, 2, NLATH, slot_total, 2, 2)
    scaling = quad_weight[:, None, None] / (wave_factor(slot_pair, M)[None] * math.sqrt(NLON))
    coeffs = (sums * scaling[None, None, None, :, :, :, None]).astype(jnp.bfloat16)
    coeffs = coeffs.transpose(4, 5, 2, 0, 1, 6, 3).reshape(slot_total, 2, 2, col_total, NLATH)

    def direct_group(operands):
        legendre_part, coeff_part, mask_part = operands
        partial_sum = jnp.einsum('sij,sohci->sjohc', legendre_part.astype(jnp.float32), coeff_part.astype(jnp.float32))
        joined = jnp.einsum('sjohc,sjoh->sjc', partial_sum, mask_part, precision=lax.Precision.HIGHEST)
        return joined.astype(jnp.bfloat16)
    spectral_out = lax.map(direct_group, (legendre.reshape(-1, group_size, NLATH, row_total), coeffs.reshape(-1, group_size, 2, 2, col_total, NLATH), masks.reshape(-1, group_size, row_total, 2, 2)))
    spectral_out = spectral_out.reshape(slot_total, row_total, col_total)
    return (arrival, spectral_out)
```

```python
import functools
import math

import jax
import jax.numpy as jnp
import numpy as np
from jax import lax
from jax.experimental import pallas as pl
from jax.experimental.pallas import tpu as pltpu
from jax.sharding import PartitionSpec as P

M = 1280
NLON = 5120
FIELDS = 4
WAVES = 16
BANDS = 16
SLOTS = 40
ROWS = 88
NROW = ROWS * BANDS
LATS = 5
BAND_LATS = LATS * WAVES
Q1 = 40
Q2 = 128
M1 = 40
P2 = 16
SPAD = 48
LANES = 256
RIM = 3
MESH = pl.DeviceIdType.MESH
F32 = jnp.float32
BF16 = jnp.bfloat16
VMEM_LIMIT = 50 * 1024 * 1024
NT = (((1,), (1,)), ((), ()))
TN = (((0,), (0,)), ((), ()))


def phase_tables():
    m1 = np.arange(M1)[:, None, None]
    p2 = np.arange(P2)[None, :, None]
    q2 = np.arange(Q2)[None, None, :]
    e = np.zeros((M1, 2, 2, P2, 2, Q2))
    for o, m in enumerate((m1 + M1 * p2, m1 + M1 * (31 - p2))):
        a = 2 * np.pi * ((m * q2) % NLON) / NLON
        e[:, o, 0, :, 0] = np.cos(a)
        e[:, o, 0, :, 1] = np.sin(a)
        e[:, o, 1, :, 0] = -np.sin(a)
        e[:, o, 1, :, 1] = np.cos(a)
    a = 2 * np.pi * (np.outer(np.arange(Q1), np.arange(M1)) % M1) / M1
    t = np.zeros((Q1, 2, 2, 2, M1))
    for h in range(2):
        t[:, h, 0, h] = np.cos(a)
        t[:, h, 1, h] = -np.sin(a)
    t = t.reshape(Q1 * 2, 4 * M1)
    sel = np.zeros((LANES, 4, 128))
    for i in range(LATS):
        for o in range(2):
            for h in range(2):
                for f in range(FIELDS):
                    for r in range(2):
                        lane = i * 32 + ((o * 2 + h) * FIELDS + f) * 2 + r
                        sel[lane, o * 2 + r, (i * FIELDS + f) * 2 + h] = 1
    sel = sel.reshape(LANES, 512)
    return [
        v.astype(np.float32).astype(jnp.bfloat16)
        for v in (e.reshape(M1 * 64, 256), t, t.T.copy(), sel, sel.T.copy())
    ]


def exchange_kernel(axis, gather, src, dst, send_sem, recv_sem, own_sem):
    me = lax.axis_index(axis)
    count = 16
    barrier = pltpu.get_barrier_semaphore()
    for d in range(1, count):
        pl.semaphore_signal(
            barrier, inc=1, device_id={axis: lax.rem(me + d, count)}, device_id_type=MESH
        )
    pl.semaphore_wait(barrier, count - 1)
    copies = []
    for d in range(1, count):
        peer = lax.rem(me + d, count)
        copy = pltpu.make_async_remote_copy(
            src_ref=src if gather else src.at[peer],
            dst_ref=dst.at[me],
            send_sem=send_sem.at[d],
            recv_sem=recv_sem.at[d],
            device_id={axis: peer},
            device_id_type=MESH,
        )
        copy.start()
        copies.append(copy)
    own = pltpu.make_async_copy(src if gather else src.at[me], dst.at[me], own_sem)
    own.start()
    own.wait()
    for copy in copies:
        copy.wait()


def exchange(x, axis, gather, cid):
    shape = ((16,) + x.shape) if gather else x.shape
    return pl.pallas_call(
        functools.partial(exchange_kernel, axis, gather),
        out_shape=jax.ShapeDtypeStruct(shape, x.dtype),
        in_specs=[pl.BlockSpec(memory_space=pl.ANY)],
        out_specs=pl.BlockSpec(memory_space=pl.ANY),
        scratch_shapes=[
            pltpu.SemaphoreType.DMA((16,)),
            pltpu.SemaphoreType.DMA((16,)),
            pltpu.SemaphoreType.DMA,
        ],
        compiler_params=pltpu.CompilerParams(collective_id=cid, has_side_effects=True),
    )(x)


def halo_kernel(grid, before, after, send_sem, recv_sem):
    band, wave = lax.axis_index("band"), lax.axis_index("wave")
    rank = band * WAVES + wave
    total = BANDS * WAVES
    nxt, prv = lax.rem(rank + 1, total), lax.rem(rank + total - 1, total)
    ids = [{"band": r // WAVES, "wave": lax.rem(r, WAVES)} for r in (nxt, prv)]
    barrier = pltpu.get_barrier_semaphore()
    for where in ids:
        pl.semaphore_signal(barrier, inc=1, device_id=where, device_id_type=MESH)
    pl.semaphore_wait(barrier, 2)
    copies = []
    for k, (src, dst) in enumerate(((grid.at[pl.ds(2, RIM)], before), (grid.at[pl.ds(0, RIM)], after))):
        copy = pltpu.make_async_remote_copy(
            src_ref=src,
            dst_ref=dst,
            send_sem=send_sem.at[k],
            recv_sem=recv_sem.at[k],
            device_id=ids[k],
            device_id_type=MESH,
        )
        copy.start()
        copies.append(copy)
    for copy in copies:
        copy.wait()


def halo(grid, cid):
    shape = jax.ShapeDtypeStruct((RIM,) + grid.shape[1:], grid.dtype)
    return pl.pallas_call(
        halo_kernel,
        out_shape=(shape, shape),
        in_specs=[pl.BlockSpec(memory_space=pl.ANY)],
        out_specs=(pl.BlockSpec(memory_space=pl.ANY),) * 2,
        scratch_shapes=[pltpu.SemaphoreType.DMA((2,)), pltpu.SemaphoreType.DMA((2,))],
        compiler_params=pltpu.CompilerParams(collective_id=cid, has_side_effects=True),
    )(grid)


GROUP = 4


def row_marks(pair, shape):
    j = lax.broadcasted_iota(jnp.int32, shape, 1)
    low_count = M - pair
    higher = j >= low_count
    degree = jnp.where(higher, j - low_count, j)
    sign = (1 - 2 * (degree & 1)).astype(F32)
    return higher, jnp.where(j <= M, 1.0, 0.0), sign


def to_latitude_kernel(pairs, spec, leg, out, rows, held):
    g = pl.program_id(0)
    for b in range(BANDS):
        rows[:, ROWS * b : ROWS * (b + 1)] = spec[b].astype(F32)[:, :ROWS]
    for k in range(GROUP):
        s = g * GROUP + k
        pair = pairs[s]
        value = rows[8 * k : 8 * k + 8, :]
        higher, used, sign = row_marks(pair, (8, NROW))
        value = value * used
        low = jnp.where(higher, 0.0, value) * jnp.where(pair == 0, 1.0, 2.0)
        high = jnp.where(higher, value, 0.0) * 2.0
        x = jnp.concatenate([low, low * sign, high, high * sign], axis=0).astype(BF16)
        held[pl.ds(BAND_LATS * s, BAND_LATS), 0:32] = lax.dot_general(
            leg[k], x, NT, preferred_element_type=F32
        )

    @pl.when(g == SLOTS // GROUP - 1)
    def _():
        for w in range(WAVES):
            part = [held[pl.ds(LATS * w + i, SLOTS, stride=BAND_LATS), :][:, 0:32] for i in range(LATS)]
            first = jnp.concatenate(part[:4], axis=1)
            second = jnp.concatenate([part[4], jnp.zeros((SLOTS, 96), F32)], axis=1)
            both = jnp.concatenate([first, second], axis=1)
            both = jnp.concatenate([both, jnp.zeros((SPAD - SLOTS, LANES), F32)], axis=0)
            out[w] = both.astype(BF16)


def to_latitude(pairs, spec, leg):
    return pl.pallas_call(
        to_latitude_kernel,
        grid=(SLOTS // GROUP,),
        out_shape=jax.ShapeDtypeStruct((WAVES, SPAD, LANES), BF16),
        in_specs=[
            pl.BlockSpec(memory_space=pltpu.SMEM),
            pl.BlockSpec((BANDS, 8 * GROUP, 128), lambda g: (0, g, 0)),
            pl.BlockSpec((GROUP, BAND_LATS, NROW), lambda g: (g, 0, 0)),
        ],
        out_specs=pl.BlockSpec((WAVES, SPAD, LANES), lambda g: (0, 0, 0)),
        scratch_shapes=[pltpu.VMEM((8 * GROUP, NROW), F32), pltpu.VMEM((SLOTS * BAND_LATS, 128), F32)],
        compiler_params=pltpu.CompilerParams(vmem_limit_bytes=VMEM_LIMIT),
    )(pairs, spec, leg)


def to_degree_kernel(pairs, coef, leg, out, held):
    g = pl.program_id(0)

    @pl.when(g == 0)
    def _():
        for w in range(WAVES):
            block = coef[w].astype(F32)
            for i in range(LATS):
                held[pl.ds(LATS * w + i, SLOTS, stride=BAND_LATS), :] = jnp.concatenate(
                    [block[:SLOTS, 32 * i : 32 * i + 32], jnp.zeros((SLOTS, 96), F32)], axis=1
                )

    for k in range(GROUP):
        s = g * GROUP + k
        mine = held[pl.ds(BAND_LATS * s, BAND_LATS), :][:, 0:32].astype(BF16)
        both = lax.dot_general(mine, leg[k], TN, preferred_element_type=F32)
        higher, used, sign = row_marks(pairs[s], (8, NROW))
        low = both[0:8] + sign * both[8:16]
        high = both[16:24] + sign * both[24:32]
        total = jnp.where(higher, high, low) * used
        for b in range(BANDS):
            out[b, 8 * k : 8 * k + 8, :] = jnp.concatenate(
                [total[:, ROWS * b : ROWS * (b + 1)], jnp.zeros((8, 128 - ROWS), F32)], axis=1
            ).astype(BF16)


def to_degree(pairs, coef, leg):
    return pl.pallas_call(
        to_degree_kernel,
        grid=(SLOTS // GROUP,),
        out_shape=jax.ShapeDtypeStruct((BANDS, 8 * SLOTS, 128), BF16),
        in_specs=[
            pl.BlockSpec(memory_space=pltpu.SMEM),
            pl.BlockSpec((WAVES, SPAD, LANES), lambda g: (0, 0, 0)),
            pl.BlockSpec((GROUP, BAND_LATS, NROW), lambda g: (g, 0, 0)),
        ],
        out_specs=pl.BlockSpec((BANDS, 8 * GROUP, 128), lambda g: (0, g, 0)),
        scratch_shapes=[pltpu.VMEM((SLOTS * BAND_LATS, 128), F32)],
        compiler_params=pltpu.CompilerParams(vmem_limit_bytes=VMEM_LIMIT),
    )(pairs, coef, leg)


def to_grid_kernel(place, four, phase, dft, sel, grid, by_pair, mixed):
    row = lax.broadcasted_iota(jnp.int32, (640, WAVES * SPAD), 0)
    onehot = jnp.where(row == place[...], 1.0, 0.0).astype(BF16)
    ordered = jnp.dot(onehot, four[...], preferred_element_type=F32).astype(BF16)
    by_pair[...] = jnp.dot(ordered, sel[...], preferred_element_type=F32).astype(BF16)
    for m1 in range(M1):
        low, high = pl.ds(P2 * m1, P2), pl.ds(P2 * (M1 - 1 - m1), P2)
        left = jnp.concatenate(
            [by_pair[low, 0:128], by_pair[low, 128:256], by_pair[high, 256:384], by_pair[high, 384:512]],
            axis=0,
        )
        part = lax.dot_general(left, phase[64 * m1 : 64 * m1 + 64, :], TN, preferred_element_type=F32)
        mixed[pl.ds(m1, 40, stride=M1), :] = part[0:40, 0:128]
        mixed[pl.ds(1600 + m1, 40, stride=M1), :] = part[0:40, 128:256]
    for n in range(LATS * FIELDS):
        right = jnp.concatenate(
            [mixed[80 * n : 80 * n + 80, :], mixed[1600 + 80 * n : 1680 + 80 * n, :]], axis=0
        ).astype(BF16)
        grid[n // FIELDS, n % FIELDS] = jnp.dot(dft[...], right, preferred_element_type=F32).astype(BF16)


def whole(n):
    return [pl.BlockSpec(memory_space=pltpu.VMEM)] * n


def to_grid(place, four, phase, dft, sel):
    return pl.pallas_call(
        to_grid_kernel,
        out_shape=jax.ShapeDtypeStruct((LATS, FIELDS, 80, Q2), BF16),
        in_specs=whole(5),
        out_specs=whole(1)[0],
        scratch_shapes=[pltpu.VMEM((640, 512), BF16), pltpu.VMEM((3200, 128), F32)],
        compiler_params=pltpu.CompilerParams(vmem_limit_bytes=VMEM_LIMIT),
    )(place, four, phase, dft, sel)


def shifted(x, by, lane):
    if by == 0:
        return x
    if by > 0:
        carried = jnp.concatenate([x[2:], x[:2]], axis=0)
        return pltpu.roll(jnp.where(lane < by, carried, x), Q2 - by, 1)
    carried = jnp.concatenate([x[78:], x[:78]], axis=0)
    return pltpu.roll(jnp.where(lane >= Q2 + by, carried, x), -by, 1)


def spread(values, bit, step):
    n = len(values)
    out = []
    for k in range(n + step):
        keep = values[k] if k < n else 0.0
        moved = values[k - step] if k >= step else 0.0
        out.append(jnp.where(bit, moved, keep))
    return out


def stencil_kernel(
    rank, grid, before, after, code, pick, weight, quad, place, phase, dft_back, sel_back,
    arrival, back, ext, moved, summed, mixed, by_pair,
):
    lane = lax.broadcasted_iota(jnp.int32, (80, Q2), 1)
    row_odd = (lax.broadcasted_iota(jnp.int32, (80, Q2), 0) & 1) == 1
    for f in range(FIELDS):
        for i in range(LATS):
            ext[RIM + i, f] = grid[i, f].astype(F32)
        for k in range(RIM):
            ext[k, f] = before[k, f].astype(F32)
            ext[RIM + LATS + k, f] = after[k, f].astype(F32)

    @pl.when(rank[0] == 0)
    def _():
        for f in range(FIELDS):
            for k in range(RIM):
                x = grid[RIM - 1 - k, f].astype(F32)
                ext[k, f] = jnp.concatenate([x[40:], x[:40]], axis=0)

    @pl.when(rank[0] == BANDS * WAVES - 1)
    def _():
        for f in range(FIELDS):
            for k in range(RIM):
                x = grid[LATS - 1 - k, f].astype(F32)
                up = jnp.concatenate([x[1:], x[:1]], axis=0)
                down = jnp.concatenate([x[79:], x[:79]], axis=0)
                ext[RIM + LATS + k, f] = jnp.where(row_odd, down, up)

    def shift_row(n, _):
        x = ext[n // FIELDS, lax.rem(n, FIELDS)]
        for c in range(7):
            moved[c, n // FIELDS, lax.rem(n, FIELDS)] = shifted(x, c - 3, lane)
        return 0

    lax.fori_loop(0, (LATS + 2 * RIM) * FIELDS, shift_row, 0)

    def chunk(n, _):
        i, start = n // 10, pl.multiple_of(lax.rem(n, 10) * 8, 8)
        at = pl.multiple_of(n * 8, 8)
        e = code[pl.ds(at, 8), :]
        t = pick[pl.ds(at, 8), :]
        taps = [
            jnp.take_along_axis(jnp.broadcast_to(weight[k : k + 1, :], (8, 128)), t, axis=1)
            for k in range(16)
        ]
        x0, x1 = (e & 1) == 1, (e & 2) == 2
        y0, y1 = (e & 4) == 4, (e & 8) == 8
        columns = [spread([taps[4 * a + b] for a in range(4)], y0, 1) for b in range(4)]
        columns = [spread(column, y1, 2) for column in columns]
        total = [jnp.zeros((8, 128), F32) for _ in range(FIELDS)]
        for sr in range(7):
            factors = spread(spread([columns[b][sr] for b in range(4)], x0, 1), x1, 2)
            for sc in range(7):
                for f in range(FIELDS):
                    total[f] = total[f] + factors[sc] * moved[sc, i + sr, f, pl.ds(start, 8), :]
        for f in range(FIELDS):
            summed[i, f, pl.ds(start, 8), :] = total[f]
        return 0

    lax.fori_loop(0, 50, chunk, 0)
    for n in range(LATS * FIELDS):
        i, f = n // FIELDS, n % FIELDS
        value = summed[i, f].astype(BF16)
        arrival[f, 80 * i : 80 * i + 80, :] = value
        both = jnp.dot(dft_back[...], value, preferred_element_type=F32)
        mixed[80 * n : 80 * n + 80, :] = both[0:80]
        mixed[1600 + 80 * n : 1680 + 80 * n, :] = both[80:160]
    by_pair[...] = jnp.zeros((640, 512), BF16)
    for m1 in range(M1):
        right = jnp.concatenate(
            [mixed[pl.ds(m1, 40, stride=M1), :], mixed[pl.ds(1600 + m1, 40, stride=M1), :]], axis=1
        ).astype(BF16)
        part = lax.dot_general(phase[64 * m1 : 64 * m1 + 64, :], right, NT, preferred_element_type=F32)
        part = (part * quad[:, 0:40]).astype(BF16)
        low, high = pl.ds(P2 * m1, P2), pl.ds(P2 * (M1 - 1 - m1), P2)
        for k, where in enumerate((low, low, high, high)):
            by_pair[where, 128 * k : 128 * k + 40] = part[16 * k : 16 * k + 16]
    ordered = jnp.dot(by_pair[...], sel_back[...], preferred_element_type=F32).astype(BF16)
    column = lax.broadcasted_iota(jnp.int32, (WAVES * SPAD, 640), 1)
    onehot = jnp.where(column == place[...], 1.0, 0.0).astype(BF16)
    back[...] = jnp.dot(onehot, ordered, preferred_element_type=F32).astype(BF16)


def stencil(rank, grid, before, after, code, pick, weight, quad, place, phase, dft_back, sel_back):
    return pl.pallas_call(
        stencil_kernel,
        out_shape=(
            jax.ShapeDtypeStruct((FIELDS, 2 * LATS * Q1, Q2), BF16),
            jax.ShapeDtypeStruct((WAVES * SPAD, LANES), BF16),
        ),
        in_specs=[pl.BlockSpec(memory_space=pltpu.SMEM)] + whole(11),
        out_specs=tuple(whole(2)),
        scratch_shapes=[
            pltpu.VMEM((LATS + 2 * RIM, FIELDS, 80, Q2), F32),
            pltpu.VMEM((7, LATS + 2 * RIM, FIELDS, 80, Q2), F32),
            pltpu.VMEM((LATS, FIELDS, 80, Q2), F32),
            pltpu.VMEM((3200, 128), F32),
            pltpu.VMEM((640, 512), BF16),
        ],
        compiler_params=pltpu.CompilerParams(vmem_limit_bytes=VMEM_LIMIT),
    )(rank, grid, before, after, code, pick, weight, quad, place, phase, dft_back, sel_back)


def grid_view(x):
    return x.reshape(2, LATS, Q1, Q2).transpose(1, 2, 0, 3).reshape(2 * LATS * Q1, Q2)


def per_device(
    spectral, legendre, slot_pair, quad_weight, depart_code, stencil_pick, stencil_weight
):
    phase, dft, dft_back, sel, sel_back = [jnp.asarray(t) for t in phase_tables()]
    wave_rank = lax.axis_index("wave")
    band_rank = lax.axis_index("band")
    pairs = lax.dynamic_slice_in_dim(slot_pair, wave_rank * SLOTS, SLOTS)
    place = (slot_pair % M1) * P2 + slot_pair // M1
    place = jnp.pad(place.reshape(WAVES, SLOTS), ((0, 0), (0, SPAD - SLOTS)), constant_values=-1)
    rank = (band_rank * WAVES + wave_rank).reshape(1)
    my_weight = lax.dynamic_slice_in_dim(quad_weight, wave_rank * LATS, LATS)
    quad = jnp.repeat(my_weight / math.sqrt(NLON), 2 * FIELDS)
    quad = jnp.pad(quad, (0, 128 - quad.shape[0])).reshape(1, 128)
    weight = jnp.pad(stencil_weight.T, ((0, 0), (0, 112)))

    own = spectral.transpose(0, 2, 1).reshape(8 * SLOTS, ROWS)
    own = jnp.pad(own, ((0, 0), (0, 128 - ROWS)))
    spec = exchange(own, "band", True, 1)
    four = to_latitude(pairs, spec, legendre)
    four = exchange(four, "wave", False, 2)
    grid = to_grid(place.reshape(1, -1), four.reshape(WAVES * SPAD, LANES), phase, dft, sel)
    before, after = halo(grid, 3)
    arrival, back = stencil(
        rank, grid, before, after, grid_view(depart_code), grid_view(stencil_pick), weight, quad,
        place.reshape(-1, 1), phase, dft_back, sel_back,
    )
    back = exchange(back.reshape(WAVES, SPAD, LANES), "wave", False, 4)
    parts = to_degree(pairs, back, legendre)
    parts = exchange(parts, "band", False, 5)
    total = jnp.sum(parts.astype(F32), axis=0).astype(BF16)
    spectral_out = total.reshape(SLOTS, 8, 128)[:, :, :ROWS].transpose(0, 2, 1)
    arrival = arrival.reshape(FIELDS, LATS, Q1, 2, Q2).transpose(0, 3, 1, 2, 4)
    return arrival.reshape(1, FIELDS, 2, LATS, NLON), spectral_out


def solution(mesh):
    lat = ("band", "wave")
    in_specs = (
        P("wave", "band", None),
        P("wave", "band", None),
        P(),
        P("band"),
        P(None, None, lat, None),
        P(None, None, lat, None),
        P(),
    )
    out_specs = (P(None, None, None, lat, None), P("wave", "band", None))
    return jax.shard_map(
        per_device, mesh=mesh, in_specs=in_specs, out_specs=out_specs, check_vma=False
    )
```

```python
import functools
import math

import jax
import jax.numpy as jnp
import numpy as np
from jax import lax
from jax.experimental import pallas as pl
from jax.experimental.pallas import tpu as pltpu
from jax.sharding import PartitionSpec as P

M = 1280
NLON = 5120
FIELDS = 4
WAVES = 16
BANDS = 16
SLOTS = 40
ROWS = 88
NROW = ROWS * BANDS
LATS = 5
BAND_LATS = LATS * WAVES
Q1 = 40
Q2 = 128
M1 = 40
P2 = 16
LANES = 256
RIM = 3
MESH = pl.DeviceIdType.MESH
F32 = jnp.float32
BF16 = jnp.bfloat16
VMEM_LIMIT = 50 * 1024 * 1024
NT = (((1,), (1,)), ((), ()))
TN = (((0,), (0,)), ((), ()))


def phase_tables():
    m1 = np.arange(M1)[:, None, None]
    p2 = np.arange(P2)[None, :, None]
    q2 = np.arange(Q2)[None, None, :]
    e = np.zeros((M1, 2, 2, P2, 2, Q2))
    for o, m in enumerate((m1 + M1 * p2, m1 + M1 * (31 - p2))):
        a = 2 * np.pi * ((m * q2) % NLON) / NLON
        e[:, o, 0, :, 0] = np.cos(a)
        e[:, o, 0, :, 1] = np.sin(a)
        e[:, o, 1, :, 0] = -np.sin(a)
        e[:, o, 1, :, 1] = np.cos(a)
    a = 2 * np.pi * (np.outer(np.arange(Q1), np.arange(M1)) % M1) / M1
    t = np.zeros((Q1, 2, 2, 2, M1))
    for h in range(2):
        t[:, h, 0, h] = np.cos(a)
        t[:, h, 1, h] = -np.sin(a)
    t = t.reshape(Q1 * 2, 4 * M1)
    sel = np.zeros((LANES, 4, 128))
    for i in range(LATS):
        for o in range(2):
            for h in range(2):
                for f in range(FIELDS):
                    for r in range(2):
                        lane = i * 32 + ((o * 2 + h) * FIELDS + f) * 2 + r
                        sel[lane, o * 2 + r, (i * FIELDS + f) * 2 + h] = 1
    sel = sel.reshape(LANES, 512)
    return [
        v.astype(np.float32).astype(jnp.bfloat16)
        for v in (e.reshape(M1 * 64, 256), t, t.T.copy(), sel, sel.T.copy())
    ]


GROUPS = 5
GROUP = SLOTS // GROUPS
TALL = 8 * GROUP
SIDE = 4


def row_marks(pair, shape):
    j = lax.broadcasted_iota(jnp.int32, shape, 1)
    low_count = M - pair
    higher = j >= low_count
    degree = jnp.where(higher, j - low_count, j)
    sign = (1 - 2 * (degree & 1)).astype(F32)
    return higher, jnp.where(j <= M, 1.0, 0.0), sign


class Plane:
    def __init__(self, g):
        band = lax.axis_index("band")
        x, y = band // SIDE, lax.rem(band, SIDE)
        self.x_first = g % 2 == 0
        self.d = 1 if (g // 2) % 2 == 0 else -1
        self.u, self.v = (x, y) if self.x_first else (y, x)

    def step(self, at, by):
        return lax.rem(at + by + SIDE, SIDE)

    def along_u(self, by):
        u = self.step(self.u, by)
        return {"band": u * SIDE + self.v if self.x_first else self.v * SIDE + u}

    def along_v(self, by):
        v = self.step(self.v, by)
        return {"band": self.u * SIDE + v if self.x_first else v * SIDE + self.u}


def greet():
    barrier = pltpu.get_barrier_semaphore()
    me = lax.axis_index("wave")
    plane = Plane(0)
    for by in (1, -1):
        for where in (plane.along_u(by), plane.along_v(by)):
            pl.semaphore_signal(barrier, inc=1, device_id=where, device_id_type=MESH)
    for d in range(1, WAVES):
        pl.semaphore_signal(
            barrier, inc=1, device_id={"wave": lax.rem(me + d, WAVES)}, device_id_type=MESH
        )
    return barrier, 4 + WAVES - 1


def remote(src, dst, send_sem, recv_sem, where):
    return pltpu.make_async_remote_copy(
        src_ref=src, dst_ref=dst, send_sem=send_sem, recv_sem=recv_sem,
        device_id=where, device_id_type=MESH,
    )


def wave_copies(src, dst, g, send_sem, recv_sem):
    me = lax.axis_index("wave")
    copies = []
    for d in range(1, WAVES):
        peer = lax.rem(me + d, WAVES)
        copies.append(
            remote(src.at[peer, g], dst.at[me, g], send_sem.at[g, d], recv_sem.at[g, d], {"wave": peer})
        )
    return copies


def forward_kernel(
    pairs, spec, leg_hbm, out,
    leg, gath, rows, held, packed, leg_sem, plane_send, plane_recv, wave_send, wave_recv,
):
    me = lax.axis_index("wave")
    barrier, greeted = greet()
    loads = [
        pltpu.make_async_copy(
            leg_hbm.at[pl.ds(GROUP * g, GROUP)], leg.at[pl.ds(GROUP * g, GROUP)], leg_sem.at[g]
        )
        for g in range(GROUPS)
    ]
    planes, hops = [], []
    for g in range(GROUPS):
        p = Plane(g)
        place = (p.u, p.v) if p.x_first else (p.v, p.u)
        gath[g, place[0], place[1]] = jnp.concatenate(
            [spec[TALL * g : TALL * (g + 1), :], jnp.zeros((TALL, 128 - ROWS), BF16)], axis=1
        )

        def one(u, g=g, p=p):
            return gath.at[g, u, p.v] if p.x_first else gath.at[g, p.v, u]

        def line(v, g=g, p=p):
            return gath.at[g, :, v] if p.x_first else gath.at[g, v]

        own, passed = one(p.u), one(p.step(p.u, -p.d))
        full, through = line(p.v), line(p.step(p.v, -p.d))
        plan = (
            (own, p.along_u(1)), (own, p.along_u(-1)), (passed, p.along_u(p.d)),
            (full, p.along_v(1)), (full, p.along_v(-1)), (through, p.along_v(p.d)),
        )
        hops.append(
            [remote(r, r, plane_send.at[g, k], plane_recv.at[g, k], w) for k, (r, w) in enumerate(plan)]
        )
        planes.append(p)
    for load in loads:
        load.start()
    pl.semaphore_wait(barrier, greeted)
    for g in range(GROUPS):
        hops[g][0].start()
        hops[g][1].start()

    sent = []

    def multiply(g):
        for b in range(BANDS):
            rows[:, ROWS * b : ROWS * (b + 1)] = gath[g, b // SIDE, b % SIDE].astype(F32)[:, :ROWS]

        def slots(part, _):
            for k in range(4):
                at = part * 4 + k
                s = GROUP * g + at
                pair = pairs[s]
                value = rows[pl.ds(pl.multiple_of(8 * at, 8), 8), :]
                higher, used, sign = row_marks(pair, (8, NROW))
                value = value * used
                low = jnp.where(higher, 0.0, value) * jnp.where(pair == 0, 1.0, 2.0)
                high = jnp.where(higher, value, 0.0) * 2.0
                x = jnp.concatenate([low, low * sign, high, high * sign], axis=0).astype(BF16)
                held[pl.ds(pl.multiple_of(BAND_LATS * at, 16), BAND_LATS), 0:32] = lax.dot_general(
                    leg[s], x, NT, preferred_element_type=F32
                )
            return 0

        lax.fori_loop(0, GROUP // 4, slots, 0)
        for w in range(WAVES):
            part = [held[pl.ds(LATS * w + i, GROUP, stride=BAND_LATS), :][:, 0:32] for i in range(LATS)]
            first = jnp.concatenate(part[:4], axis=1)
            second = jnp.concatenate([part[4], jnp.zeros((GROUP, 96), F32)], axis=1)
            packed[w, g] = jnp.concatenate([first, second], axis=0).astype(BF16)
        copies = wave_copies(packed, out, g, wave_send, wave_recv)
        for copy in copies:
            copy.start()
        out[me, g] = packed[me, g]
        sent.extend(copies)

    for t in range(GROUPS + 3):
        g = t - 2
        if 0 <= g < GROUPS:
            hops[g][3 if planes[g].d == 1 else 4].wait_recv()
            hops[g][5].start()
        g = t - 1
        if 0 <= g < GROUPS:
            hops[g][1 if planes[g].d == 1 else 0].wait_recv()
            hops[g][2].wait_recv()
            hops[g][3].start()
            hops[g][4].start()
        g = t
        if 0 <= g < GROUPS:
            hops[g][0 if planes[g].d == 1 else 1].wait_recv()
            hops[g][2].start()
        g = t - 3
        if 0 <= g < GROUPS:
            hops[g][4 if planes[g].d == 1 else 3].wait_recv()
            hops[g][5].wait_recv()
            loads[g].wait()
            multiply(g)
    for group in hops:
        for hop in group:
            hop.wait_send()
    for copy in sent:
        copy.wait()


def forward(pairs, spec, leg):
    return pl.pallas_call(
        forward_kernel,
        out_shape=jax.ShapeDtypeStruct((WAVES, GROUPS, 16, 128), BF16),
        in_specs=[
            pl.BlockSpec(memory_space=pltpu.SMEM),
            pl.BlockSpec(memory_space=pltpu.VMEM),
            pl.BlockSpec(memory_space=pl.ANY),
        ],
        out_specs=pl.BlockSpec(memory_space=pltpu.VMEM),
        scratch_shapes=[
            pltpu.VMEM((SLOTS, BAND_LATS, NROW), BF16),
            pltpu.VMEM((GROUPS, SIDE, SIDE, TALL, 128), BF16),
            pltpu.VMEM((TALL, NROW), F32),
            pltpu.VMEM((GROUP * BAND_LATS, 128), F32),
            pltpu.VMEM((WAVES, GROUPS, 16, 128), BF16),
            pltpu.SemaphoreType.DMA((GROUPS,)),
            pltpu.SemaphoreType.DMA((GROUPS, 6)),
            pltpu.SemaphoreType.DMA((GROUPS, 6)),
            pltpu.SemaphoreType.DMA((GROUPS, WAVES)),
            pltpu.SemaphoreType.DMA((GROUPS, WAVES)),
        ],
        compiler_params=pltpu.CompilerParams(
            collective_id=1, has_side_effects=True, vmem_limit_bytes=VMEM_LIMIT
        ),
    )(pairs, spec, leg)


def backward_kernel(
    pairs, coef, leg_hbm, out,
    leg, recv, held, tall, part, first, relay, line, line_out, second, relay_out,
    leg_sem, wave_send, wave_recv, plane_send, plane_recv,
):
    me = lax.axis_index("wave")
    barrier, greeted = greet()
    loads = [
        pltpu.make_async_copy(
            leg_hbm.at[pl.ds(GROUP * g, GROUP)], leg.at[pl.ds(GROUP * g, GROUP)], leg_sem.at[g]
        )
        for g in range(GROUPS)
    ]
    for load in loads:
        load.start()
    planes, hops = [], []
    for g in range(GROUPS):
        p = Plane(g)

        def towards(u, g=g, p=p):
            return part.at[g, u] if p.x_first else part.at[g, :, u]

        plan = (
            (towards(p.step(p.u, 2)), first.at[g, 0], p.along_u(p.d)),
            (towards(p.step(p.u, -p.d)), first.at[g, 1], p.along_u(-p.d)),
            (relay.at[g], first.at[g, 2], p.along_u(p.d)),
            (line_out.at[g, p.step(p.v, 2)], second.at[g, 0], p.along_v(p.d)),
            (line_out.at[g, p.step(p.v, -p.d)], second.at[g, 1], p.along_v(-p.d)),
            (relay_out.at[g], second.at[g, 2], p.along_v(p.d)),
        )
        hops.append(
            [
                remote(a, b, plane_send.at[g, k], plane_recv.at[g, k], w)
                for k, (a, b, w) in enumerate(plan)
            ]
        )
        planes.append(p)
    pl.semaphore_wait(barrier, greeted)
    waves = [wave_copies(coef, recv, g, wave_send, wave_recv) for g in range(GROUPS)]
    for copies in waves:
        for copy in copies:
            copy.start()
    recv[me] = coef[me]

    def mine(g, u):
        return (part[g, u] if planes[g].x_first else part[g, :, u]).astype(F32)

    def multiply(g):
        for w in range(WAVES):
            block = recv[w, g].astype(F32)
            for i in range(LATS):
                value = block[8:16] if i == 4 else block[0:8]
                if 0 < i < 4:
                    value = pltpu.roll(value, 128 - 32 * i, 1)
                held[pl.ds(LATS * w + i, GROUP, stride=BAND_LATS), :] = value

        def slots(piece, _):
            for k in range(4):
                at = piece * 4 + k
                s = GROUP * g + at
                lats = held[pl.ds(pl.multiple_of(BAND_LATS * at, 16), BAND_LATS), :][:, 0:32]
                both = lax.dot_general(lats.astype(BF16), leg[s], TN, preferred_element_type=F32)
                higher, used, sign = row_marks(pairs[s], (8, NROW))
                low = both[0:8] + sign * both[8:16]
                high = both[16:24] + sign * both[24:32]
                tall[pl.ds(pl.multiple_of(8 * at, 8), 8), :] = jnp.where(higher, high, low) * used
            return 0

        lax.fori_loop(0, GROUP // 4, slots, 0)
        for b in range(BANDS):
            part[g, b // SIDE, b % SIDE] = jnp.concatenate(
                [tall[:, ROWS * b : ROWS * (b + 1)], jnp.zeros((TALL, 128 - ROWS), F32)], axis=1
            ).astype(BF16)

    for t in range(GROUPS + 4):
        g = t
        if 0 <= g < GROUPS:
            for copy in waves[g]:
                copy.wait_recv()
            loads[g].wait()
            multiply(g)
            hops[g][0].start()
            hops[g][1].start()
        g = t - 1
        if 0 <= g < GROUPS:
            p = planes[g]
            hops[g][0].wait_recv()
            relay[g] = (first[g, 0].astype(F32) + mine(g, p.step(p.u, p.d))).astype(BF16)
            hops[g][2].start()
        g = t - 2
        if 0 <= g < GROUPS:
            p = planes[g]
            hops[g][1].wait_recv()
            hops[g][2].wait_recv()
            line[g] = mine(g, p.u) + first[g, 1].astype(F32) + first[g, 2].astype(F32)
            line_out[g] = line[g].astype(BF16)
            hops[g][3].start()
            hops[g][4].start()
        g = t - 3
        if 0 <= g < GROUPS:
            p = planes[g]
            hops[g][3].wait_recv()
            relay_out[g] = (second[g, 0].astype(F32) + line[g, p.step(p.v, p.d)]).astype(BF16)
            hops[g][5].start()
        g = t - 4
        if 0 <= g < GROUPS:
            p = planes[g]
            hops[g][4].wait_recv()
            hops[g][5].wait_recv()
            out[TALL * g : TALL * (g + 1), :] = (
                line[g, p.v] + second[g, 1].astype(F32) + second[g, 2].astype(F32)
            ).astype(BF16)
    for group in hops:
        for hop in group:
            hop.wait_send()
    for copies in waves:
        for copy in copies:
            copy.wait_send()


def backward(pairs, coef, leg):
    return pl.pallas_call(
        backward_kernel,
        out_shape=jax.ShapeDtypeStruct((8 * SLOTS, 128), BF16),
        in_specs=[
            pl.BlockSpec(memory_space=pltpu.SMEM),
            pl.BlockSpec(memory_space=pltpu.VMEM),
            pl.BlockSpec(memory_space=pl.ANY),
        ],
        out_specs=pl.BlockSpec(memory_space=pltpu.VMEM),
        scratch_shapes=[
            pltpu.VMEM((SLOTS, BAND_LATS, NROW), BF16),
            pltpu.VMEM((WAVES, GROUPS, 16, 128), BF16),
            pltpu.VMEM((GROUP * BAND_LATS, 128), F32),
            pltpu.VMEM((TALL, NROW), F32),
            pltpu.VMEM((GROUPS, SIDE, SIDE, TALL, 128), BF16),
            pltpu.VMEM((GROUPS, 3, SIDE, TALL, 128), BF16),
            pltpu.VMEM((GROUPS, SIDE, TALL, 128), BF16),
            pltpu.VMEM((GROUPS, SIDE, TALL, 128), F32),
            pltpu.VMEM((GROUPS, SIDE, TALL, 128), BF16),
            pltpu.VMEM((GROUPS, 3, TALL, 128), BF16),
            pltpu.VMEM((GROUPS, TALL, 128), BF16),
            pltpu.SemaphoreType.DMA((GROUPS,)),
            pltpu.SemaphoreType.DMA((GROUPS, WAVES)),
            pltpu.SemaphoreType.DMA((GROUPS, WAVES)),
            pltpu.SemaphoreType.DMA((GROUPS, 6)),
            pltpu.SemaphoreType.DMA((GROUPS, 6)),
        ],
        compiler_params=pltpu.CompilerParams(
            collective_id=2, has_side_effects=True, vmem_limit_bytes=VMEM_LIMIT
        ),
    )(pairs, coef, leg)


def to_grid_kernel(place, four, phase, dft, sel, grid, by_pair, mixed, send_sem, recv_sem):
    rank = lax.axis_index("band") * WAVES + lax.axis_index("wave")
    total = BANDS * WAVES
    ends = (lax.rem(rank + 1, total), lax.rem(rank + total - 1, total))
    ids = [{"band": r // WAVES, "wave": lax.rem(r, WAVES)} for r in ends]
    barrier = pltpu.get_barrier_semaphore()
    for where in ids:
        pl.semaphore_signal(barrier, inc=1, device_id=where, device_id_type=MESH)
    row = lax.broadcasted_iota(jnp.int32, (640, 640), 0)
    onehot = jnp.where(row == place[...], 1.0, 0.0).astype(BF16)
    blocks = four[...].astype(F32)
    slots = jnp.concatenate(
        [blocks[:, :, 0:8].reshape(640, 128), blocks[:, :, 8:16].reshape(640, 128)], axis=1
    ).astype(BF16)
    ordered = jnp.dot(onehot, slots, preferred_element_type=F32).astype(BF16)
    by_pair[...] = jnp.dot(ordered, sel[...], preferred_element_type=F32).astype(BF16)
    for m1 in range(M1):
        low, high = pl.ds(P2 * m1, P2), pl.ds(P2 * (M1 - 1 - m1), P2)
        left = jnp.concatenate(
            [by_pair[low, 0:128], by_pair[low, 128:256], by_pair[high, 256:384], by_pair[high, 384:512]],
            axis=0,
        )
        part = lax.dot_general(left, phase[64 * m1 : 64 * m1 + 64, :], TN, preferred_element_type=F32)
        mixed[pl.ds(m1, 40, stride=M1), :] = part[0:40, 0:128]
        mixed[pl.ds(1600 + m1, 40, stride=M1), :] = part[0:40, 128:256]
    for n in range(LATS * FIELDS):
        right = jnp.concatenate(
            [mixed[80 * n : 80 * n + 80, :], mixed[1600 + 80 * n : 1680 + 80 * n, :]], axis=0
        ).astype(BF16)
        grid[RIM + n // FIELDS, n % FIELDS] = jnp.dot(
            dft[...], right, preferred_element_type=F32
        ).astype(BF16)
    pl.semaphore_wait(barrier, 2)
    copies = [
        remote(grid.at[pl.ds(a, RIM)], grid.at[pl.ds(b, RIM)], send_sem.at[k], recv_sem.at[k], ids[k])
        for k, (a, b) in enumerate(((LATS, 0), (RIM, RIM + LATS)))
    ]
    for copy in copies:
        copy.start()
    for copy in copies:
        copy.wait()


def whole(n):
    return [pl.BlockSpec(memory_space=pltpu.VMEM)] * n


def to_grid(place, four, phase, dft, sel):
    return pl.pallas_call(
        to_grid_kernel,
        out_shape=jax.ShapeDtypeStruct((LATS + 2 * RIM, FIELDS, 80, Q2), BF16),
        in_specs=whole(5),
        out_specs=whole(1)[0],
        scratch_shapes=[
            pltpu.VMEM((640, 512), BF16),
            pltpu.VMEM((3200, 128), F32),
            pltpu.SemaphoreType.DMA((2,)),
            pltpu.SemaphoreType.DMA((2,)),
        ],
        compiler_params=pltpu.CompilerParams(
            collective_id=3, has_side_effects=True, vmem_limit_bytes=VMEM_LIMIT
        ),
    )(place, four, phase, dft, sel)


def shifted(x, by, lane):
    if by == 0:
        return x
    if by > 0:
        carried = jnp.concatenate([x[2:], x[:2]], axis=0)
        return pltpu.roll(jnp.where(lane < by, carried, x), Q2 - by, 1)
    carried = jnp.concatenate([x[78:], x[:78]], axis=0)
    return pltpu.roll(jnp.where(lane >= Q2 + by, carried, x), -by, 1)


def spread(values, bit, step):
    n = len(values)
    out = []
    for k in range(n + step):
        keep = values[k] if k < n else 0.0
        moved = values[k - step] if k >= step else 0.0
        out.append(jnp.where(bit, moved, keep))
    return out


def stencil_kernel(
    rank, grid, code, pick, weight, quad, place, phase, dft_back, sel_back,
    arrival, back, ext, moved, summed, mixed, by_pair,
):
    lane = lax.broadcasted_iota(jnp.int32, (80, Q2), 1)
    row_odd = (lax.broadcasted_iota(jnp.int32, (80, Q2), 0) & 1) == 1
    for f in range(FIELDS):
        for i in range(LATS):
            ext[RIM + i, f] = grid[RIM + i, f].astype(F32)
        for k in range(RIM):
            ext[k, f] = grid[k, f].astype(F32)
            ext[RIM + LATS + k, f] = grid[RIM + LATS + k, f].astype(F32)

    @pl.when(rank[0] == 0)
    def _():
        for f in range(FIELDS):
            for k in range(RIM):
                x = grid[2 * RIM - 1 - k, f].astype(F32)
                ext[k, f] = jnp.concatenate([x[40:], x[:40]], axis=0)

    @pl.when(rank[0] == BANDS * WAVES - 1)
    def _():
        for f in range(FIELDS):
            for k in range(RIM):
                x = grid[RIM + LATS - 1 - k, f].astype(F32)
                up = jnp.concatenate([x[1:], x[:1]], axis=0)
                down = jnp.concatenate([x[79:], x[:79]], axis=0)
                ext[RIM + LATS + k, f] = jnp.where(row_odd, down, up)

    def shift_row(n, _):
        x = ext[n // FIELDS, lax.rem(n, FIELDS)]
        for c in range(7):
            moved[c, n // FIELDS, lax.rem(n, FIELDS)] = shifted(x, c - 3, lane)
        return 0

    lax.fori_loop(0, (LATS + 2 * RIM) * FIELDS, shift_row, 0)

    def chunk(n, _):
        i, start = n // 10, pl.multiple_of(lax.rem(n, 10) * 8, 8)
        at = pl.multiple_of(n * 8, 8)
        e = code[pl.ds(at, 8), :]
        t = pick[pl.ds(at, 8), :]
        taps = [
            jnp.take_along_axis(jnp.broadcast_to(weight[k : k + 1, :], (8, 128)), t, axis=1)
            for k in range(16)
        ]
        x0, x1 = (e & 1) == 1, (e & 2) == 2
        y0, y1 = (e & 4) == 4, (e & 8) == 8
        columns = [spread([taps[4 * a + b] for a in range(4)], y0, 1) for b in range(4)]
        columns = [spread(column, y1, 2) for column in columns]
        total = [jnp.zeros((8, 128), F32) for _ in range(FIELDS)]
        for sr in range(7):
            factors = spread(spread([columns[b][sr] for b in range(4)], x0, 1), x1, 2)
            for sc in range(7):
                for f in range(FIELDS):
                    total[f] = total[f] + factors[sc] * moved[sc, i + sr, f, pl.ds(start, 8), :]
        for f in range(FIELDS):
            summed[i, f, pl.ds(start, 8), :] = total[f]
        return 0

    lax.fori_loop(0, 50, chunk, 0)
    for n in range(LATS * FIELDS):
        i, f = n // FIELDS, n % FIELDS
        value = summed[i, f].astype(BF16)
        arrival[f, 80 * i : 80 * i + 80, :] = value
        both = jnp.dot(dft_back[...], value, preferred_element_type=F32)
        mixed[80 * n : 80 * n + 80, :] = both[0:80]
        mixed[1600 + 80 * n : 1680 + 80 * n, :] = both[80:160]
    by_pair[...] = jnp.zeros((640, 512), BF16)
    for m1 in range(M1):
        right = jnp.concatenate(
            [mixed[pl.ds(m1, 40, stride=M1), :], mixed[pl.ds(1600 + m1, 40, stride=M1), :]], axis=1
        ).astype(BF16)
        part = lax.dot_general(phase[64 * m1 : 64 * m1 + 64, :], right, NT, preferred_element_type=F32)
        part = (part * quad[:, 0:40]).astype(BF16)
        low, high = pl.ds(P2 * m1, P2), pl.ds(P2 * (M1 - 1 - m1), P2)
        for k, where in enumerate((low, low, high, high)):
            by_pair[where, 128 * k : 128 * k + 40] = part[16 * k : 16 * k + 16]
    ordered = jnp.dot(by_pair[...], sel_back[...], preferred_element_type=F32).astype(BF16)
    column = lax.broadcasted_iota(jnp.int32, (640, 640), 1)
    onehot = jnp.where(column == place[...], 1.0, 0.0).astype(BF16)
    slots = jnp.dot(onehot, ordered, preferred_element_type=F32)
    back[...] = jnp.concatenate(
        [slots[:, 0:128].reshape(80, 8, 128), slots[:, 128:256].reshape(80, 8, 128)], axis=1
    ).astype(BF16).reshape(WAVES, GROUPS, 16, 128)


def stencil(rank, grid, code, pick, weight, quad, place, phase, dft_back, sel_back):
    return pl.pallas_call(
        stencil_kernel,
        out_shape=(
            jax.ShapeDtypeStruct((FIELDS, 2 * LATS * Q1, Q2), BF16),
            jax.ShapeDtypeStruct((WAVES, GROUPS, 16, 128), BF16),
        ),
        in_specs=[pl.BlockSpec(memory_space=pltpu.SMEM)] + whole(9),
        out_specs=tuple(whole(2)),
        scratch_shapes=[
            pltpu.VMEM((LATS + 2 * RIM, FIELDS, 80, Q2), F32),
            pltpu.VMEM((7, LATS + 2 * RIM, FIELDS, 80, Q2), F32),
            pltpu.VMEM((LATS, FIELDS, 80, Q2), F32),
            pltpu.VMEM((3200, 128), F32),
            pltpu.VMEM((640, 512), BF16),
        ],
        compiler_params=pltpu.CompilerParams(vmem_limit_bytes=VMEM_LIMIT),
    )(rank, grid, code, pick, weight, quad, place, phase, dft_back, sel_back)


def grid_view(x):
    return x.reshape(2, LATS, Q1, Q2).transpose(1, 2, 0, 3).reshape(2 * LATS * Q1, Q2)


def per_device(
    spectral, legendre, slot_pair, quad_weight, depart_code, stencil_pick, stencil_weight
):
    phase, dft, dft_back, sel, sel_back = [jnp.asarray(t) for t in phase_tables()]
    wave_rank = lax.axis_index("wave")
    band_rank = lax.axis_index("band")
    pairs = lax.dynamic_slice_in_dim(slot_pair, wave_rank * SLOTS, SLOTS)
    place = (slot_pair % M1) * P2 + slot_pair // M1
    rank = (band_rank * WAVES + wave_rank).reshape(1)
    my_weight = lax.dynamic_slice_in_dim(quad_weight, wave_rank * LATS, LATS)
    quad = jnp.repeat(my_weight / math.sqrt(NLON), 2 * FIELDS)
    quad = jnp.pad(quad, (0, 128 - quad.shape[0])).reshape(1, 128)
    weight = jnp.pad(stencil_weight.T, ((0, 0), (0, 112)))

    own = spectral.transpose(0, 2, 1).reshape(8 * SLOTS, ROWS)
    four = forward(pairs, own, legendre)
    grid = to_grid(place.reshape(1, -1), four, phase, dft, sel)
    arrival, back = stencil(
        rank, grid, grid_view(depart_code), grid_view(stencil_pick), weight, quad,
        place.reshape(-1, 1), phase, dft_back, sel_back,
    )
    total = backward(pairs, back, legendre)
    spectral_out = total.reshape(SLOTS, 8, 128)[:, :, :ROWS].transpose(0, 2, 1)
    arrival = arrival.reshape(FIELDS, LATS, Q1, 2, Q2).transpose(0, 3, 1, 2, 4)
    return arrival.reshape(1, FIELDS, 2, LATS, NLON), spectral_out


def solution(mesh):
    lat = ("band", "wave")
    in_specs = (
        P("wave", "band", None),
        P("wave", "band", None),
        P(),
        P("band"),
        P(None, None, lat, None),
        P(None, None, lat, None),
        P(),
    )
    out_specs = (P(None, None, None, lat, None), P("wave", "band", None))
    return jax.shard_map(
        per_device, mesh=mesh, in_specs=in_specs, out_specs=out_specs, check_vma=False
    )
```

```python
import functools
import math

import jax
import jax.numpy as jnp
import numpy as np
from jax import lax
from jax.experimental import pallas as pl
from jax.experimental.pallas import tpu as pltpu
from jax.sharding import PartitionSpec as P

M = 1280
NLON = 5120
FIELDS = 4
WAVES = 16
BANDS = 16
SLOTS = 40
ROWS = 88
NROW = ROWS * BANDS
LATS = 5
BAND_LATS = LATS * WAVES
Q1 = 40
Q2 = 128
M1 = 40
P2 = 16
LANES = 256
RIM = 3
MESH = pl.DeviceIdType.MESH
F32 = jnp.float32
BF16 = jnp.bfloat16
VMEM_LIMIT = 50 * 1024 * 1024
NT = (((1,), (1,)), ((), ()))
TN = (((0,), (0,)), ((), ()))


def phase_tables():
    m1 = np.arange(M1)[:, None, None]
    p2 = np.arange(P2)[None, :, None]
    q2 = np.arange(Q2)[None, None, :]
    e = np.zeros((M1, 2, 2, P2, 2, Q2))
    for o, m in enumerate((m1 + M1 * p2, m1 + M1 * (31 - p2))):
        a = 2 * np.pi * ((m * q2) % NLON) / NLON
        e[:, o, 0, :, 0] = np.cos(a)
        e[:, o, 0, :, 1] = np.sin(a)
        e[:, o, 1, :, 0] = -np.sin(a)
        e[:, o, 1, :, 1] = np.cos(a)
    a = 2 * np.pi * (np.outer(np.arange(Q1), np.arange(M1)) % M1) / M1
    t = np.zeros((Q1, 2, 2, 2, M1))
    for h in range(2):
        t[:, h, 0, h] = np.cos(a)
        t[:, h, 1, h] = -np.sin(a)
    t = t.reshape(Q1 * 2, 4 * M1)
    sel = np.zeros((LANES, 4, 128))
    for i in range(LATS):
        for o in range(2):
            for h in range(2):
                for f in range(FIELDS):
                    for r in range(2):
                        lane = i * 32 + ((o * 2 + h) * FIELDS + f) * 2 + r
                        sel[lane, o * 2 + r, (i * FIELDS + f) * 2 + h] = 1
    sel = sel.reshape(LANES, 512)
    return [
        v.astype(np.float32).astype(jnp.bfloat16)
        for v in (e.reshape(M1 * 64, 256), t, t.T.copy(), sel, sel.T.copy())
    ]


GROUPS = 5
GROUP = SLOTS // GROUPS
TALL = 8 * GROUP
HALF = TALL // 2
STEPS = (1, 3, 2)
SIDE = 4


def row_marks(pair, shape):
    j = lax.broadcasted_iota(jnp.int32, shape, 1)
    low_count = M - pair
    higher = j >= low_count
    degree = jnp.where(higher, j - low_count, j)
    sign = (1 - 2 * (degree & 1)).astype(F32)
    return higher, jnp.where(j <= M, 1.0, 0.0), sign


class Plane:
    def __init__(self, k):
        band = lax.axis_index("band")
        x, y = band // SIDE, lax.rem(band, SIDE)
        self.x_first = k == 0
        self.u, self.v = (x, y) if self.x_first else (y, x)

    def along_u(self, by):
        u = turn(self.u, by)
        return {"band": u * SIDE + self.v if self.x_first else self.v * SIDE + u}

    def along_v(self, by):
        v = turn(self.v, by)
        return {"band": self.u * SIDE + v if self.x_first else v * SIDE + self.u}


def turn(at, by):
    return lax.rem(at + by, SIDE)


def greet():
    barrier = pltpu.get_barrier_semaphore()
    me = lax.axis_index("wave")
    plane = Plane(0)
    for by in (1, 3, 2):
        for where in (plane.along_u(by), plane.along_v(by)):
            pl.semaphore_signal(barrier, inc=1, device_id=where, device_id_type=MESH)
    for d in range(1, WAVES):
        pl.semaphore_signal(
            barrier, inc=1, device_id={"wave": lax.rem(me + d, WAVES)}, device_id_type=MESH
        )
    return barrier, 6 + WAVES - 1


def remote(src, dst, send_sem, recv_sem, where):
    return pltpu.make_async_remote_copy(
        src_ref=src, dst_ref=dst, send_sem=send_sem, recv_sem=recv_sem,
        device_id=where, device_id_type=MESH,
    )


def wave_copies(src, dst, g, send_sem, recv_sem):
    me = lax.axis_index("wave")
    copies = []
    for d in range(1, WAVES):
        peer = lax.rem(me + d, WAVES)
        copies.append(
            remote(src.at[peer, g], dst.at[me, g], send_sem.at[g, d], recv_sem.at[g, d], {"wave": peer})
        )
    return copies


def forward_kernel(
    pairs, spec, leg_hbm, out,
    leg, gath, rows, held, packed, leg_sem, plane_send, plane_recv, wave_send, wave_recv,
):
    me = lax.axis_index("wave")
    barrier, greeted = greet()
    loads = [
        pltpu.make_async_copy(
            leg_hbm.at[pl.ds(GROUP * g, GROUP)], leg.at[pl.ds(GROUP * g, GROUP)], leg_sem.at[g]
        )
        for g in range(GROUPS)
    ]
    near, far = [], []
    for g in range(GROUPS):
        for k in range(2):
            p = Plane(k)
            start = TALL * g + HALF * k
            own = jnp.concatenate(
                [spec[start : start + HALF, :], jnp.zeros((HALF, 128 - ROWS), BF16)], axis=1
            )
            if k == 0:
                gath[g, 0, p.u, p.v] = own
                one, line = gath.at[g, 0, p.u, p.v], gath.at[g, 0, :, p.v]
            else:
                gath[g, 1, p.v, p.u] = own
                one, line = gath.at[g, 1, p.v, p.u], gath.at[g, 1, p.v]
            for n, by in enumerate(STEPS):
                near.append(
                    remote(one, one, plane_send.at[g, k, n], plane_recv.at[g, k, n], p.along_u(by))
                )
                far.append(
                    remote(
                        line, line, plane_send.at[g, k, 3 + n], plane_recv.at[g, k, 3 + n], p.along_v(by)
                    )
                )
    pl.semaphore_wait(barrier, greeted)
    for hop in near:
        hop.start()
    for load in loads:
        load.start()

    sent = []

    def multiply(g):
        for b in range(BANDS):
            for k in range(2):
                rows[HALF * k : HALF * (k + 1), ROWS * b : ROWS * (b + 1)] = gath[
                    g, k, b // SIDE, b % SIDE
                ].astype(F32)[:, :ROWS]

        def slots(part, _):
            for k in range(4):
                at = part * 4 + k
                s = GROUP * g + at
                pair = pairs[me * SLOTS + s]
                value = rows[pl.ds(pl.multiple_of(8 * at, 8), 8), :]
                higher, used, sign = row_marks(pair, (8, NROW))
                value = value * used
                low = jnp.where(higher, 0.0, value) * jnp.where(pair == 0, 1.0, 2.0)
                high = jnp.where(higher, value, 0.0) * 2.0
                x = jnp.concatenate([low, low * sign, high, high * sign], axis=0).astype(BF16)
                held[pl.ds(pl.multiple_of(BAND_LATS * at, 16), BAND_LATS), 0:32] = lax.dot_general(
                    leg[s], x, NT, preferred_element_type=F32
                )
            return 0

        lax.fori_loop(0, GROUP // 4, slots, 0)
        for w in range(WAVES):
            part = [held[pl.ds(LATS * w + i, GROUP, stride=BAND_LATS), :][:, 0:32] for i in range(LATS)]
            first = jnp.concatenate(part[:4], axis=1)
            second = jnp.concatenate([part[4], jnp.zeros((GROUP, 96), F32)], axis=1)
            packed[w, g] = jnp.concatenate([first, second], axis=0).astype(BF16)
        copies = wave_copies(packed, out, g, wave_send, wave_recv)
        for copy in copies:
            copy.start()
        out[me, g] = packed[me, g]
        sent.extend(copies)

    for g in range(GROUPS):
        for k in range(6):
            near[6 * g + k].wait_recv()
        for k in range(6):
            far[6 * g + k].start()
    for g in range(GROUPS):
        for k in range(6):
            far[6 * g + k].wait_recv()
        loads[g].wait()
        multiply(g)
    for hop in near + far:
        hop.wait_send()
    for copy in sent:
        copy.wait()


def forward(pairs, spec, leg):
    return pl.pallas_call(
        forward_kernel,
        out_shape=jax.ShapeDtypeStruct((WAVES, GROUPS, 16, 128), BF16),
        in_specs=[
            pl.BlockSpec(memory_space=pltpu.SMEM),
            pl.BlockSpec(memory_space=pltpu.VMEM),
            pl.BlockSpec(memory_space=pl.ANY),
        ],
        out_specs=pl.BlockSpec(memory_space=pltpu.VMEM),
        scratch_shapes=[
            pltpu.VMEM((SLOTS, BAND_LATS, NROW), BF16),
            pltpu.VMEM((GROUPS, 2, SIDE, SIDE, HALF, 128), BF16),
            pltpu.VMEM((TALL, NROW), F32),
            pltpu.VMEM((GROUP * BAND_LATS, 128), F32),
            pltpu.VMEM((WAVES, GROUPS, 16, 128), BF16),
            pltpu.SemaphoreType.DMA((GROUPS,)),
            pltpu.SemaphoreType.DMA((GROUPS, 2, 6)),
            pltpu.SemaphoreType.DMA((GROUPS, 2, 6)),
            pltpu.SemaphoreType.DMA((GROUPS, WAVES)),
            pltpu.SemaphoreType.DMA((GROUPS, WAVES)),
        ],
        compiler_params=pltpu.CompilerParams(
            collective_id=1, has_side_effects=True, vmem_limit_bytes=VMEM_LIMIT
        ),
    )(pairs, spec, leg)


def backward_kernel(
    pairs, coef, leg_hbm, out,
    leg, recv, held, tall, part, first, line, line_out, second,
    leg_sem, wave_send, wave_recv, plane_send, plane_recv,
):
    me = lax.axis_index("wave")
    barrier, greeted = greet()
    loads = [
        pltpu.make_async_copy(
            leg_hbm.at[pl.ds(GROUP * g, GROUP)], leg.at[pl.ds(GROUP * g, GROUP)], leg_sem.at[g]
        )
        for g in range(GROUPS)
    ]
    for load in loads:
        load.start()
    near, far = [], []
    for g in range(GROUPS):
        for k in range(2):
            p = Plane(k)
            for n, by in enumerate(STEPS):
                u, v = turn(p.u, by), turn(p.v, by)
                src = part.at[g, 0, u] if k == 0 else part.at[g, 1, :, u]
                near.append(
                    remote(
                        src, first.at[g, k, n], plane_send.at[g, k, n], plane_recv.at[g, k, n], p.along_u(by)
                    )
                )
                far.append(
                    remote(
                        line_out.at[g, k, v], second.at[g, k, n],
                        plane_send.at[g, k, 3 + n], plane_recv.at[g, k, 3 + n], p.along_v(by),
                    )
                )
    pl.semaphore_wait(barrier, greeted)
    waves = [wave_copies(coef, recv, g, wave_send, wave_recv) for g in range(GROUPS)]
    for copies in waves:
        for copy in copies:
            copy.start()
    recv[me] = coef[me]

    def multiply(g):
        for w in range(WAVES):
            block = recv[w, g].astype(F32)
            for i in range(LATS):
                value = block[8:16] if i == 4 else block[0:8]
                if 0 < i < 4:
                    value = pltpu.roll(value, 128 - 32 * i, 1)
                held[pl.ds(LATS * w + i, GROUP, stride=BAND_LATS), :] = value

        def slots(piece, _):
            for k in range(4):
                at = piece * 4 + k
                s = GROUP * g + at
                lats = held[pl.ds(pl.multiple_of(BAND_LATS * at, 16), BAND_LATS), :][:, 0:32]
                both = lax.dot_general(lats.astype(BF16), leg[s], TN, preferred_element_type=F32)
                higher, used, sign = row_marks(pairs[me * SLOTS + s], (8, NROW))
                low = both[0:8] + sign * both[8:16]
                high = both[16:24] + sign * both[24:32]
                tall[pl.ds(pl.multiple_of(8 * at, 8), 8), :] = jnp.where(higher, high, low) * used
            return 0

        lax.fori_loop(0, GROUP // 4, slots, 0)
        for b in range(BANDS):
            both = jnp.concatenate(
                [tall[:, ROWS * b : ROWS * (b + 1)], jnp.zeros((TALL, 128 - ROWS), F32)], axis=1
            ).astype(BF16)
            for k in range(2):
                part[g, k, b // SIDE, b % SIDE] = both[HALF * k : HALF * (k + 1)]

    for t in range(GROUPS + 2):
        g = t
        if 0 <= g < GROUPS:
            for copy in waves[g]:
                copy.wait_recv()
            loads[g].wait()
            multiply(g)
            for k in range(6):
                near[6 * g + k].start()
        g = t - 1
        if 0 <= g < GROUPS:
            for k in range(2):
                p = Plane(k)
                total = (part[g, 0, p.u] if k == 0 else part[g, 1, :, p.u]).astype(F32)
                for n in range(3):
                    near[6 * g + 3 * k + n].wait_recv()
                    total = total + first[g, k, n].astype(F32)
                line[g, k] = total
                line_out[g, k] = total.astype(BF16)
                for n in range(3):
                    far[6 * g + 3 * k + n].start()
        g = t - 2
        if 0 <= g < GROUPS:
            for k in range(2):
                total = line[g, k, Plane(k).v]
                for n in range(3):
                    far[6 * g + 3 * k + n].wait_recv()
                    total = total + second[g, k, n].astype(F32)
                start = TALL * g + HALF * k
                out[start : start + HALF, :] = total.astype(BF16)
    for hop in near + far:
        hop.wait_send()
    for copies in waves:
        for copy in copies:
            copy.wait_send()


def backward(pairs, coef, leg):
    return pl.pallas_call(
        backward_kernel,
        out_shape=jax.ShapeDtypeStruct((8 * SLOTS, 128), BF16),
        in_specs=[
            pl.BlockSpec(memory_space=pltpu.SMEM),
            pl.BlockSpec(memory_space=pltpu.VMEM),
            pl.BlockSpec(memory_space=pl.ANY),
        ],
        out_specs=pl.BlockSpec(memory_space=pltpu.VMEM),
        scratch_shapes=[
            pltpu.VMEM((SLOTS, BAND_LATS, NROW), BF16),
            pltpu.VMEM((WAVES, GROUPS, 16, 128), BF16),
            pltpu.VMEM((GROUP * BAND_LATS, 128), F32),
            pltpu.VMEM((TALL, NROW), F32),
            pltpu.VMEM((GROUPS, 2, SIDE, SIDE, HALF, 128), BF16),
            pltpu.VMEM((GROUPS, 2, 3, SIDE, HALF, 128), BF16),
            pltpu.VMEM((GROUPS, 2, SIDE, HALF, 128), F32),
            pltpu.VMEM((GROUPS, 2, SIDE, HALF, 128), BF16),
            pltpu.VMEM((GROUPS, 2, 3, HALF, 128), BF16),
            pltpu.SemaphoreType.DMA((GROUPS,)),
            pltpu.SemaphoreType.DMA((GROUPS, WAVES)),
            pltpu.SemaphoreType.DMA((GROUPS, WAVES)),
            pltpu.SemaphoreType.DMA((GROUPS, 2, 6)),
            pltpu.SemaphoreType.DMA((GROUPS, 2, 6)),
        ],
        compiler_params=pltpu.CompilerParams(
            collective_id=2, has_side_effects=True, vmem_limit_bytes=VMEM_LIMIT
        ),
    )(pairs, coef, leg)


def to_grid_kernel(place, four, phase, dft, sel, grid, by_pair, mixed, send_sem, recv_sem):
    rank = lax.axis_index("band") * WAVES + lax.axis_index("wave")
    total = BANDS * WAVES
    ends = (lax.rem(rank + 1, total), lax.rem(rank + total - 1, total))
    ids = [{"band": r // WAVES, "wave": lax.rem(r, WAVES)} for r in ends]
    barrier = pltpu.get_barrier_semaphore()
    for where in ids:
        pl.semaphore_signal(barrier, inc=1, device_id=where, device_id_type=MESH)
    row = lax.broadcasted_iota(jnp.int32, (640, 640), 0)
    onehot = jnp.where(row == order_of(place[...]), 1.0, 0.0).astype(BF16)
    blocks = four[...].astype(F32)
    slots = jnp.concatenate(
        [blocks[:, :, 0:8].reshape(640, 128), blocks[:, :, 8:16].reshape(640, 128)], axis=1
    ).astype(BF16)
    ordered = jnp.dot(onehot, slots, preferred_element_type=F32).astype(BF16)
    by_pair[...] = jnp.dot(ordered, sel[...], preferred_element_type=F32).astype(BF16)
    for m1 in range(M1):
        low, high = pl.ds(P2 * m1, P2), pl.ds(P2 * (M1 - 1 - m1), P2)
        left = jnp.concatenate(
            [by_pair[low, 0:128], by_pair[low, 128:256], by_pair[high, 256:384], by_pair[high, 384:512]],
            axis=0,
        )
        part = lax.dot_general(left, phase[64 * m1 : 64 * m1 + 64, :], TN, preferred_element_type=F32)
        mixed[pl.ds(m1, 40, stride=M1), :] = part[0:40, 0:128]
        mixed[pl.ds(1600 + m1, 40, stride=M1), :] = part[0:40, 128:256]
    for n in range(LATS * FIELDS):
        right = jnp.concatenate(
            [mixed[80 * n : 80 * n + 80, :], mixed[1600 + 80 * n : 1680 + 80 * n, :]], axis=0
        ).astype(BF16)
        grid[RIM + n // FIELDS, n % FIELDS] = jnp.dot(
            dft[...], right, preferred_element_type=F32
        ).astype(BF16)
    pl.semaphore_wait(barrier, 2)
    copies = [
        remote(grid.at[pl.ds(a, RIM)], grid.at[pl.ds(b, RIM)], send_sem.at[k], recv_sem.at[k], ids[k])
        for k, (a, b) in enumerate(((LATS, 0), (RIM, RIM + LATS)))
    ]
    for copy in copies:
        copy.start()
    for copy in copies:
        copy.wait()


def order_of(pair):
    p2 = (pair * 1639) >> 16
    return (pair - M1 * p2) * P2 + p2


def whole(n):
    return [pl.BlockSpec(memory_space=pltpu.VMEM)] * n


def to_grid(place, four, phase, dft, sel):
    return pl.pallas_call(
        to_grid_kernel,
        out_shape=jax.ShapeDtypeStruct((LATS + 2 * RIM, FIELDS, 80, Q2), BF16),
        in_specs=whole(5),
        out_specs=whole(1)[0],
        scratch_shapes=[
            pltpu.VMEM((640, 512), BF16),
            pltpu.VMEM((3200, 128), F32),
            pltpu.SemaphoreType.DMA((2,)),
            pltpu.SemaphoreType.DMA((2,)),
        ],
        compiler_params=pltpu.CompilerParams(
            collective_id=3, has_side_effects=True, vmem_limit_bytes=VMEM_LIMIT
        ),
    )(place, four, phase, dft, sel)


def spread(values, bit, step):
    n = len(values)
    out = []
    for k in range(n + step):
        keep = values[k] if k < n else 0.0
        moved = values[k - step] if k >= step else 0.0
        out.append(jnp.where(bit, moved, keep))
    return out


def stencil_kernel(
    rank, grid, code, pick, weight, quad, place, phase, dft_back, sel_back,
    arrival, back, ext, moved, summed, mixed, by_pair, taps_of, shifts, shifts2,
):
    wave = lax.axis_index("wave")
    lat = lax.broadcasted_iota(jnp.int32, (1, 40), 1) // (2 * FIELDS)
    scale = jnp.zeros((1, 40), F32)
    for i in range(LATS):
        scale = jnp.where(lat == i, quad[wave * LATS + i] / math.sqrt(NLON), scale)
    wide = jnp.concatenate([weight[...], jnp.zeros((16, 112), F32)], axis=1)
    taps_of[...] = jnp.concatenate([wide, jnp.zeros((112, 128), F32)], axis=0).T[0:16]
    row_odd = (lax.broadcasted_iota(jnp.int32, (80, Q2), 0) & 1) == 1
    for f in range(FIELDS):
        for i in range(LATS):
            ext[RIM + i, f] = grid[RIM + i, f].astype(F32)
        for k in range(RIM):
            ext[k, f] = grid[k, f].astype(F32)
            ext[RIM + LATS + k, f] = grid[RIM + LATS + k, f].astype(F32)

    @pl.when(rank[0] == 0)
    def _():
        for f in range(FIELDS):
            for k in range(RIM):
                x = grid[2 * RIM - 1 - k, f].astype(F32)
                ext[k, f] = jnp.concatenate([x[40:], x[:40]], axis=0)

    @pl.when(rank[0] == BANDS * WAVES - 1)
    def _():
        for f in range(FIELDS):
            for k in range(RIM):
                x = grid[RIM + LATS - 1 - k, f].astype(F32)
                up = jnp.concatenate([x[1:], x[:1]], axis=0)
                down = jnp.concatenate([x[79:], x[:79]], axis=0)
                ext[RIM + LATS + k, f] = jnp.where(row_odd, down, up)

    def shift_row(r, _):
        for f in range(FIELDS):
            x = ext[r, f]
            moved[3, r, f] = x
            up = jnp.concatenate([x[2:], x[:2]], axis=0)
            down = jnp.concatenate([x[78:], x[:78]], axis=0)
            both = jnp.concatenate([x, up, down], axis=1).astype(BF16)
            ahead = jnp.dot(both[:, 0:256], shifts[...], preferred_element_type=F32)
            behind = jnp.dot(
                jnp.concatenate([both[:, 0:128], both[:, 256:384]], axis=1),
                shifts2[...],
                preferred_element_type=F32,
            )
            for c in range(3):
                moved[4 + c, r, f] = ahead[:, 128 * c : 128 * c + 128]
                moved[c, r, f] = behind[:, 128 * c : 128 * c + 128]
        return 0

    rowi = lax.broadcasted_iota(jnp.int32, (256, 384), 0)
    coli = lax.broadcasted_iota(jnp.int32, (256, 384), 1)
    by = coli // 128 + 1
    want = (coli & 127) + by
    shifts[...] = jnp.where(rowi == want, 1.0, 0.0).astype(BF16)
    by = coli // 128 - 3
    want = (coli & 127) + by
    want = jnp.where(want < 0, want + 256, want)
    shifts2[...] = jnp.where(rowi == want, 1.0, 0.0).astype(BF16)
    lax.fori_loop(0, LATS + 2 * RIM, shift_row, 0, unroll=11)

    def chunk(n, _):
        i, start = n // 10, pl.multiple_of(lax.rem(n, 10) * 8, 8)
        at = pl.multiple_of(n * 8, 8)
        e = code[pl.ds(at, 8), :]
        t = pick[pl.ds(at, 8), :]
        taps = [
            jnp.take_along_axis(jnp.broadcast_to(taps_of[k : k + 1, :], (8, 128)), t, axis=1)
            for k in range(16)
        ]
        x0, x1 = (e & 1) == 1, (e & 2) == 2
        y0, y1 = (e & 4) == 4, (e & 8) == 8
        columns = [spread([taps[4 * a + b] for a in range(4)], y0, 1) for b in range(4)]
        columns = [spread(column, y1, 2) for column in columns]
        total = [jnp.zeros((8, 128), F32) for _ in range(FIELDS)]
        for sr in range(7):
            factors = spread(spread([columns[b][sr] for b in range(4)], x0, 1), x1, 2)
            for sc in range(7):
                for f in range(FIELDS):
                    total[f] = total[f] + factors[sc] * moved[sc, i + sr, f, pl.ds(start, 8), :]
        for f in range(FIELDS):
            summed[i, f, pl.ds(start, 8), :] = total[f]
        return 0

    lax.fori_loop(0, 50, chunk, 0, unroll=10)
    for n in range(LATS * FIELDS):
        i, f = n // FIELDS, n % FIELDS
        value = summed[i, f].astype(BF16)
        arrival[f, 80 * i : 80 * i + 80, :] = value
        both = jnp.dot(dft_back[...], value, preferred_element_type=F32)
        mixed[80 * n : 80 * n + 80, :] = both[0:80]
        mixed[1600 + 80 * n : 1680 + 80 * n, :] = both[80:160]
    by_pair[...] = jnp.zeros((640, 512), BF16)
    for m1 in range(M1):
        right = jnp.concatenate(
            [mixed[pl.ds(m1, 40, stride=M1), :], mixed[pl.ds(1600 + m1, 40, stride=M1), :]], axis=1
        ).astype(BF16)
        part = lax.dot_general(phase[64 * m1 : 64 * m1 + 64, :], right, NT, preferred_element_type=F32)
        part = (part * scale).astype(BF16)
        low, high = pl.ds(P2 * m1, P2), pl.ds(P2 * (M1 - 1 - m1), P2)
        for k, where in enumerate((low, low, high, high)):
            by_pair[where, 128 * k : 128 * k + 40] = part[16 * k : 16 * k + 16]
    ordered = jnp.dot(by_pair[...], sel_back[...], preferred_element_type=F32).astype(BF16)
    column = lax.broadcasted_iota(jnp.int32, (640, 640), 1)
    onehot = jnp.where(column == order_of(place[...]), 1.0, 0.0).astype(BF16)
    slots = jnp.dot(onehot, ordered, preferred_element_type=F32)
    back[...] = jnp.concatenate(
        [slots[:, 0:128].reshape(80, 8, 128), slots[:, 128:256].reshape(80, 8, 128)], axis=1
    ).astype(BF16).reshape(WAVES, GROUPS, 16, 128)


def stencil(rank, grid, code, pick, weight, quad, place, phase, dft_back, sel_back):
    smem = pl.BlockSpec(memory_space=pltpu.SMEM)
    return pl.pallas_call(
        stencil_kernel,
        out_shape=(
            jax.ShapeDtypeStruct((FIELDS, 2 * LATS * Q1, Q2), BF16),
            jax.ShapeDtypeStruct((WAVES, GROUPS, 16, 128), BF16),
        ),
        in_specs=[smem] + whole(4) + [smem] + whole(4),
        out_specs=tuple(whole(2)),
        scratch_shapes=[
            pltpu.VMEM((LATS + 2 * RIM, FIELDS, 80, Q2), F32),
            pltpu.VMEM((7, LATS + 2 * RIM, FIELDS, 80, Q2), F32),
            pltpu.VMEM((LATS, FIELDS, 80, Q2), F32),
            pltpu.VMEM((3200, 128), F32),
            pltpu.VMEM((640, 512), BF16),
            pltpu.VMEM((16, 128), F32),
            pltpu.VMEM((256, 384), BF16),
            pltpu.VMEM((256, 384), BF16),
        ],
        compiler_params=pltpu.CompilerParams(vmem_limit_bytes=VMEM_LIMIT),
    )(rank, grid, code, pick, weight, quad, place, phase, dft_back, sel_back)


def grid_view(x):
    return x.reshape(2, LATS, Q1, Q2).transpose(1, 2, 0, 3).reshape(2 * LATS * Q1, Q2)


def per_device(
    spectral, legendre, slot_pair, quad_weight, depart_code, stencil_pick, stencil_weight
):
    phase, dft, dft_back, sel, sel_back = [jnp.asarray(t) for t in phase_tables()]
    wave_rank = lax.axis_index("wave")
    band_rank = lax.axis_index("band")
    pairs = slot_pair
    rank = (band_rank * WAVES + wave_rank).reshape(1)
    own = spectral.transpose(0, 2, 1).reshape(8 * SLOTS, ROWS)
    four = forward(pairs, own, legendre)
    grid = to_grid(slot_pair.reshape(1, -1), four, phase, dft, sel)
    arrival, back = stencil(
        rank, grid, grid_view(depart_code), grid_view(stencil_pick), stencil_weight, quad_weight,
        slot_pair.reshape(-1, 1), phase, dft_back, sel_back,
    )
    total = backward(pairs, back, legendre)
    spectral_out = total.reshape(SLOTS, 8, 128)[:, :, :ROWS].transpose(0, 2, 1)
    arrival = arrival.reshape(FIELDS, LATS, Q1, 2, Q2).transpose(0, 3, 1, 2, 4)
    return arrival.reshape(1, FIELDS, 2, LATS, NLON), spectral_out


def solution(mesh):
    lat = ("band", "wave")
    in_specs = (
        P("wave", "band", None),
        P("wave", "band", None),
        P(),
        P("band"),
        P(None, None, lat, None),
        P(None, None, lat, None),
        P(),
    )
    out_specs = (P(None, None, None, lat, None), P("wave", "band", None))
    return jax.shard_map(
        per_device, mesh=mesh, in_specs=in_specs, out_specs=out_specs, check_vma=False
    )
```

```python
import functools
import math

import jax
import jax.numpy as jnp
import numpy as np
from jax import lax
from jax.experimental import pallas as pl
from jax.experimental.pallas import tpu as pltpu
from jax.sharding import PartitionSpec as P

M = 1280
NLON = 5120
FIELDS = 4
WAVES = 16
BANDS = 16
SLOTS = 40
ROWS = 88
NROW = ROWS * BANDS
LATS = 5
BAND_LATS = LATS * WAVES
Q1 = 40
Q2 = 128
M1 = 40
P2 = 16
LANES = 256
RIM = 3
MESH = pl.DeviceIdType.MESH
F32 = jnp.float32
BF16 = jnp.bfloat16
VMEM_LIMIT = 50 * 1024 * 1024
NT = (((1,), (1,)), ((), ()))
TN = (((0,), (0,)), ((), ()))


def phase_tables():
    m1 = np.arange(M1)[:, None, None]
    p2 = np.arange(P2)[None, :, None]
    q2 = np.arange(Q2)[None, None, :]
    e = np.zeros((M1, 2, 2, P2, 2, Q2))
    for o, m in enumerate((m1 + M1 * p2, m1 + M1 * (31 - p2))):
        a = 2 * np.pi * ((m * q2) % NLON) / NLON
        e[:, o, 0, :, 0] = np.cos(a)
        e[:, o, 0, :, 1] = np.sin(a)
        e[:, o, 1, :, 0] = -np.sin(a)
        e[:, o, 1, :, 1] = np.cos(a)
    a = 2 * np.pi * (np.outer(np.arange(Q1), np.arange(M1)) % M1) / M1
    t = np.zeros((Q1, 2, 2, 2, M1))
    for h in range(2):
        t[:, h, 0, h] = np.cos(a)
        t[:, h, 1, h] = -np.sin(a)
    t = t.reshape(Q1 * 2, 4 * M1)
    sel = np.zeros((LANES, 4, 128))
    for i in range(LATS):
        for o in range(2):
            for h in range(2):
                for f in range(FIELDS):
                    for r in range(2):
                        lane = i * 32 + ((o * 2 + h) * FIELDS + f) * 2 + r
                        sel[lane, o * 2 + r, (i * FIELDS + f) * 2 + h] = 1
    sel = sel.reshape(LANES, 512)
    return [
        v.astype(np.float32).astype(jnp.bfloat16)
        for v in (e.reshape(M1 * 64, 256), t, t.T.copy(), sel, sel.T.copy())
    ]


GROUPS = 5
GROUP = SLOTS // GROUPS
TALL = 8 * GROUP
HALF = TALL // 2
WIDE = 384
STEPS = (1, 3, 2)
SIDE = 4


def row_marks(pair, shape):
    j = lax.broadcasted_iota(jnp.int32, shape, 1)
    low_count = M - pair
    higher = j >= low_count
    degree = jnp.where(higher, j - low_count, j)
    sign = (1 - 2 * (degree & 1)).astype(F32)
    return higher, jnp.where(j <= M, 1.0, 0.0), sign


class Plane:
    def __init__(self, k):
        band = lax.axis_index("band")
        x, y = band // SIDE, lax.rem(band, SIDE)
        self.x_first = k == 0
        self.u, self.v = (x, y) if self.x_first else (y, x)

    def along_u(self, by):
        u = turn(self.u, by)
        return {"band": u * SIDE + self.v if self.x_first else self.v * SIDE + u}

    def along_v(self, by):
        v = turn(self.v, by)
        return {"band": self.u * SIDE + v if self.x_first else v * SIDE + self.u}


def side_by_side(pieces):
    return jnp.concatenate(pieces + [jnp.zeros((8, WIDE - 4 * ROWS), F32)], axis=1).astype(BF16)


def turn(at, by):
    return lax.rem(at + by, SIDE)


def greet():
    barrier = pltpu.get_barrier_semaphore()
    me = lax.axis_index("wave")
    plane = Plane(0)
    for by in (1, 3, 2):
        for where in (plane.along_u(by), plane.along_v(by)):
            pl.semaphore_signal(barrier, inc=1, device_id=where, device_id_type=MESH)
    for d in range(1, WAVES):
        pl.semaphore_signal(
            barrier, inc=1, device_id={"wave": lax.rem(me + d, WAVES)}, device_id_type=MESH
        )
    return barrier, 6 + WAVES - 1


def remote(src, dst, send_sem, recv_sem, where):
    return pltpu.make_async_remote_copy(
        src_ref=src, dst_ref=dst, send_sem=send_sem, recv_sem=recv_sem,
        device_id=where, device_id_type=MESH,
    )


def wave_copies(src, dst, g, send_sem, recv_sem):
    me = lax.axis_index("wave")
    copies = []
    for d in range(1, WAVES):
        peer = lax.rem(me + d, WAVES)
        copies.append(
            remote(src.at[peer, g], dst.at[me, g], send_sem.at[g, d], recv_sem.at[g, d], {"wave": peer})
        )
    return copies


def forward_kernel(
    pairs, spec_hbm, leg_hbm, out,
    spec, leg, gath, rows, held, packed, leg_sem, spec_sem, plane_send, plane_recv, wave_send, wave_recv,
):
    me = lax.axis_index("wave")
    spec_load = pltpu.make_async_copy(spec_hbm, spec, spec_sem)
    spec_load.start()
    barrier, greeted = greet()
    spec_load.wait()
    loads = [
        pltpu.make_async_copy(
            leg_hbm.at[pl.ds(GROUP * g, GROUP)], leg.at[pl.ds(GROUP * g, GROUP)], leg_sem.at[g]
        )
        for g in range(GROUPS)
    ]
    near, far = [], []
    for g in range(GROUPS):
        for k in range(2):
            p = Plane(k)
            start = TALL * g + HALF * k
            own = spec[start : start + HALF, :].astype(F32)
            own = side_by_side([own[8 * m : 8 * m + 8] for m in range(4)])
            if k == 0:
                gath[g, 0, p.u, p.v] = own
                one, line = gath.at[g, 0, p.u, p.v], gath.at[g, 0, :, p.v]
            else:
                gath[g, 1, p.v, p.u] = own
                one, line = gath.at[g, 1, p.v, p.u], gath.at[g, 1, p.v]
            for n, by in enumerate(STEPS):
                near.append(
                    remote(one, one, plane_send.at[g, k, n], plane_recv.at[g, k, n], p.along_u(by))
                )
                far.append(
                    remote(
                        line, line, plane_send.at[g, k, 3 + n], plane_recv.at[g, k, 3 + n], p.along_v(by)
                    )
                )
    pl.semaphore_wait(barrier, greeted)
    for hop in near:
        hop.start()
    for load in loads:
        load.start()

    sent = []

    def multiply(g):
        for b in range(BANDS):
            for k in range(2):
                block = gath[g, k, b // SIDE, b % SIDE].astype(F32)
                for m in range(4):
                    at = HALF * k + 8 * m
                    rows[at : at + 8, ROWS * b : ROWS * (b + 1)] = block[:, ROWS * m : ROWS * (m + 1)]

        def slots(part, _):
            for k in range(4):
                at = part * 4 + k
                s = GROUP * g + at
                pair = pairs[me * SLOTS + s]
                value = rows[pl.ds(pl.multiple_of(8 * at, 8), 8), :]
                higher, used, sign = row_marks(pair, (8, NROW))
                value = value * used
                low = jnp.where(higher, 0.0, value) * jnp.where(pair == 0, 1.0, 2.0)
                high = jnp.where(higher, value, 0.0) * 2.0
                x = jnp.concatenate([low, low * sign, high, high * sign], axis=0).astype(BF16)
                held[pl.ds(pl.multiple_of(BAND_LATS * at, 16), BAND_LATS), 0:32] = lax.dot_general(
                    leg[s], x, NT, preferred_element_type=F32
                )
            return 0

        lax.fori_loop(0, GROUP // 4, slots, 0)
        for w in range(WAVES):
            part = [held[pl.ds(LATS * w + i, GROUP, stride=BAND_LATS), :][:, 0:32] for i in range(LATS)]
            first = jnp.concatenate(part[:4], axis=1)
            second = jnp.concatenate([part[4], jnp.zeros((GROUP, 96), F32)], axis=1)
            packed[w, g] = jnp.concatenate([first, second], axis=0).astype(BF16)
        copies = wave_copies(packed, out, g, wave_send, wave_recv)
        for copy in copies:
            copy.start()
        out[me, g] = packed[me, g]
        sent.extend(copies)

    for g in range(GROUPS):
        for k in range(6):
            near[6 * g + k].wait_recv()
        for k in range(6):
            far[6 * g + k].start()
    for g in range(GROUPS):
        for k in range(6):
            far[6 * g + k].wait_recv()
        loads[g].wait()
        multiply(g)
    for hop in near + far:
        hop.wait_send()
    for copy in sent:
        copy.wait()


def forward(pairs, spec, leg):
    return pl.pallas_call(
        forward_kernel,
        out_shape=jax.ShapeDtypeStruct((WAVES, GROUPS, 16, 128), BF16),
        in_specs=[
            pl.BlockSpec(memory_space=pltpu.SMEM),
            pl.BlockSpec(memory_space=pl.ANY),
            pl.BlockSpec(memory_space=pl.ANY),
        ],
        out_specs=pl.BlockSpec(memory_space=pltpu.VMEM),
        scratch_shapes=[
            pltpu.VMEM((8 * SLOTS, ROWS), BF16),
            pltpu.VMEM((SLOTS, BAND_LATS, NROW), BF16),
            pltpu.VMEM((GROUPS, 2, SIDE, SIDE, 8, WIDE), BF16),
            pltpu.VMEM((TALL, NROW), F32),
            pltpu.VMEM((GROUP * BAND_LATS, 128), F32),
            pltpu.VMEM((WAVES, GROUPS, 16, 128), BF16),
            pltpu.SemaphoreType.DMA((GROUPS,)),
            pltpu.SemaphoreType.DMA,
            pltpu.SemaphoreType.DMA((GROUPS, 2, 6)),
            pltpu.SemaphoreType.DMA((GROUPS, 2, 6)),
            pltpu.SemaphoreType.DMA((GROUPS, WAVES)),
            pltpu.SemaphoreType.DMA((GROUPS, WAVES)),
        ],
        compiler_params=pltpu.CompilerParams(
            collective_id=1, has_side_effects=True, vmem_limit_bytes=VMEM_LIMIT
        ),
    )(pairs, spec, leg)


def backward_kernel(
    pairs, coef, leg_hbm, out,
    leg, recv, held, tall, part, first, line, line_out, second,
    leg_sem, wave_send, wave_recv, plane_send, plane_recv,
):
    me = lax.axis_index("wave")
    barrier, greeted = greet()
    loads = [
        pltpu.make_async_copy(
            leg_hbm.at[pl.ds(GROUP * g, GROUP)], leg.at[pl.ds(GROUP * g, GROUP)], leg_sem.at[g]
        )
        for g in range(GROUPS)
    ]
    for load in loads:
        load.start()
    near, far = [], []
    for g in range(GROUPS):
        for k in range(2):
            p = Plane(k)
            for n, by in enumerate(STEPS):
                u, v = turn(p.u, by), turn(p.v, by)
                src = part.at[g, 0, u] if k == 0 else part.at[g, 1, :, u]
                near.append(
                    remote(
                        src, first.at[g, k, n], plane_send.at[g, k, n], plane_recv.at[g, k, n], p.along_u(by)
                    )
                )
                far.append(
                    remote(
                        line_out.at[g, k, v], second.at[g, k, n],
                        plane_send.at[g, k, 3 + n], plane_recv.at[g, k, 3 + n], p.along_v(by),
                    )
                )
    pl.semaphore_wait(barrier, greeted)
    waves = [wave_copies(coef, recv, g, wave_send, wave_recv) for g in range(GROUPS)]
    for copies in waves:
        for copy in copies:
            copy.start()
    recv[me] = coef[me]

    def multiply(g):
        for w in range(WAVES):
            block = recv[w, g].astype(F32)
            for i in range(LATS):
                value = block[8:16] if i == 4 else block[0:8]
                if 0 < i < 4:
                    value = pltpu.roll(value, 128 - 32 * i, 1)
                held[pl.ds(LATS * w + i, GROUP, stride=BAND_LATS), :] = value

        def slots(piece, _):
            for k in range(4):
                at = piece * 4 + k
                s = GROUP * g + at
                lats = held[pl.ds(pl.multiple_of(BAND_LATS * at, 16), BAND_LATS), :][:, 0:32]
                both = lax.dot_general(lats.astype(BF16), leg[s], TN, preferred_element_type=F32)
                higher, used, sign = row_marks(pairs[me * SLOTS + s], (8, NROW))
                low = both[0:8] + sign * both[8:16]
                high = both[16:24] + sign * both[24:32]
                tall[pl.ds(pl.multiple_of(8 * at, 8), 8), :] = jnp.where(higher, high, low) * used
            return 0

        lax.fori_loop(0, GROUP // 4, slots, 0)
        for b in range(BANDS):
            for k in range(2):
                part[g, k, b // SIDE, b % SIDE] = side_by_side(
                    [
                        tall[HALF * k + 8 * m : HALF * k + 8 * m + 8, ROWS * b : ROWS * (b + 1)]
                        for m in range(4)
                    ]
                )

    for g in range(GROUPS):
        for copy in waves[g]:
            copy.wait_recv()
        loads[g].wait()
        multiply(g)
        for k in range(6):
            near[6 * g + k].start()
    for g in range(GROUPS):
        for k in range(2):
            p = Plane(k)
            total = (part[g, 0, p.u] if k == 0 else part[g, 1, :, p.u]).astype(F32)
            for n in range(3):
                near[6 * g + 3 * k + n].wait_recv()
                total = total + first[g, k, n].astype(F32)
            line[g, k] = total
            line_out[g, k] = total.astype(BF16)
            for n in range(3):
                far[6 * g + 3 * k + n].start()
    for g in range(GROUPS):
        for k in range(2):
            total = line[g, k, Plane(k).v]
            for n in range(3):
                far[6 * g + 3 * k + n].wait_recv()
                total = total + second[g, k, n].astype(F32)
            start = TALL * g + HALF * k
            pieces = [
                jnp.concatenate(
                    [total[:, ROWS * m : ROWS * (m + 1)], jnp.zeros((8, 128 - ROWS), F32)], axis=1
                )
                for m in range(4)
            ]
            out[start : start + HALF, :] = jnp.concatenate(pieces, axis=0).astype(BF16)
    for hop in near + far:
        hop.wait_send()
    for copies in waves:
        for copy in copies:
            copy.wait_send()


def backward(pairs, coef, leg):
    return pl.pallas_call(
        backward_kernel,
        out_shape=jax.ShapeDtypeStruct((8 * SLOTS, 128), BF16),
        in_specs=[
            pl.BlockSpec(memory_space=pltpu.SMEM),
            pl.BlockSpec(memory_space=pltpu.VMEM),
            pl.BlockSpec(memory_space=pl.ANY),
        ],
        out_specs=pl.BlockSpec(memory_space=pltpu.VMEM),
        scratch_shapes=[
            pltpu.VMEM((SLOTS, BAND_LATS, NROW), BF16),
            pltpu.VMEM((WAVES, GROUPS, 16, 128), BF16),
            pltpu.VMEM((GROUP * BAND_LATS, 128), F32),
            pltpu.VMEM((TALL, NROW), F32),
            pltpu.VMEM((GROUPS, 2, SIDE, SIDE, 8, WIDE), BF16),
            pltpu.VMEM((GROUPS, 2, 3, SIDE, 8, WIDE), BF16),
            pltpu.VMEM((GROUPS, 2, SIDE, 8, WIDE), F32),
            pltpu.VMEM((GROUPS, 2, SIDE, 8, WIDE), BF16),
            pltpu.VMEM((GROUPS, 2, 3, 8, WIDE), BF16),
            pltpu.SemaphoreType.DMA((GROUPS,)),
            pltpu.SemaphoreType.DMA((GROUPS, WAVES)),
            pltpu.SemaphoreType.DMA((GROUPS, WAVES)),
            pltpu.SemaphoreType.DMA((GROUPS, 2, 6)),
            pltpu.SemaphoreType.DMA((GROUPS, 2, 6)),
        ],
        compiler_params=pltpu.CompilerParams(
            collective_id=2, has_side_effects=True, vmem_limit_bytes=VMEM_LIMIT
        ),
    )(pairs, coef, leg)


def to_grid_kernel(place, four, phase, dft, sel, grid, by_pair, mixed, send_sem, recv_sem):
    rank = lax.axis_index("band") * WAVES + lax.axis_index("wave")
    total = BANDS * WAVES
    ends = (lax.rem(rank + 1, total), lax.rem(rank + total - 1, total))
    ids = [{"band": r // WAVES, "wave": lax.rem(r, WAVES)} for r in ends]
    barrier = pltpu.get_barrier_semaphore()
    for where in ids:
        pl.semaphore_signal(barrier, inc=1, device_id=where, device_id_type=MESH)
    row = lax.broadcasted_iota(jnp.int32, (640, 640), 0)
    onehot = jnp.where(row == order_of(place[...].reshape(1, 640)), 1.0, 0.0).astype(BF16)
    blocks = four[...].astype(F32)
    slots = jnp.concatenate(
        [blocks[:, :, 0:8].reshape(640, 128), blocks[:, :, 8:16].reshape(640, 128)], axis=1
    ).astype(BF16)
    ordered = jnp.dot(onehot, slots, preferred_element_type=F32).astype(BF16)
    by_pair[...] = jnp.dot(ordered, sel[...], preferred_element_type=F32).astype(BF16)
    for m1 in range(M1):
        low, high = pl.ds(P2 * m1, P2), pl.ds(P2 * (M1 - 1 - m1), P2)
        left = jnp.concatenate(
            [by_pair[low, 0:128], by_pair[low, 128:256], by_pair[high, 256:384], by_pair[high, 384:512]],
            axis=0,
        )
        part = lax.dot_general(left, phase[64 * m1 : 64 * m1 + 64, :], TN, preferred_element_type=F32)
        mixed[pl.ds(m1, 40, stride=M1), :] = part[0:40, 0:128]
        mixed[pl.ds(1600 + m1, 40, stride=M1), :] = part[0:40, 128:256]
    for n in range(LATS * FIELDS):
        right = jnp.concatenate(
            [mixed[80 * n : 80 * n + 80, :], mixed[1600 + 80 * n : 1680 + 80 * n, :]], axis=0
        ).astype(BF16)
        grid[RIM + n // FIELDS, n % FIELDS] = jnp.dot(
            dft[...], right, preferred_element_type=F32
        ).astype(BF16)
    pl.semaphore_wait(barrier, 2)
    copies = [
        remote(grid.at[pl.ds(a, RIM)], grid.at[pl.ds(b, RIM)], send_sem.at[k], recv_sem.at[k], ids[k])
        for k, (a, b) in enumerate(((LATS, 0), (RIM, RIM + LATS)))
    ]
    for copy in copies:
        copy.start()
    for copy in copies:
        copy.wait()


def order_of(pair):
    p2 = (pair * 1639) >> 16
    return (pair - M1 * p2) * P2 + p2


def whole(n):
    return [pl.BlockSpec(memory_space=pltpu.VMEM)] * n


def to_grid(place, four, phase, dft, sel):
    return pl.pallas_call(
        to_grid_kernel,
        out_shape=jax.ShapeDtypeStruct((LATS + 2 * RIM, FIELDS, 80, Q2), BF16),
        in_specs=whole(5),
        out_specs=whole(1)[0],
        scratch_shapes=[
            pltpu.VMEM((640, 512), BF16),
            pltpu.VMEM((3200, 128), F32),
            pltpu.SemaphoreType.DMA((2,)),
            pltpu.SemaphoreType.DMA((2,)),
        ],
        compiler_params=pltpu.CompilerParams(
            collective_id=3, has_side_effects=True, vmem_limit_bytes=VMEM_LIMIT
        ),
    )(place, four, phase, dft, sel)


def spread(values, bit, step):
    n = len(values)
    out = []
    for k in range(n + step):
        keep = values[k] if k < n else 0.0
        moved = values[k - step] if k >= step else 0.0
        out.append(jnp.where(bit, moved, keep))
    return out


def stencil_kernel(
    rank, grid, code, pick, weight, quad, place, phase, dft_back, sel_back,
    arrival, back, ext, moved, summed, mixed, by_pair, taps_of, shifts, shifts2,
):
    wave = lax.axis_index("wave")
    lat = lax.broadcasted_iota(jnp.int32, (1, 40), 1) // (2 * FIELDS)
    scale = jnp.zeros((1, 40), F32)
    for i in range(LATS):
        scale = jnp.where(lat == i, quad[wave * LATS + i] / math.sqrt(NLON), scale)
    wide = jnp.concatenate([weight[...], jnp.zeros((16, 112), F32)], axis=1)
    taps_of[...] = jnp.concatenate([wide, jnp.zeros((112, 128), F32)], axis=0).T[0:16]
    row_odd = (lax.broadcasted_iota(jnp.int32, (80, Q2), 0) & 1) == 1
    for f in range(FIELDS):
        for i in range(LATS):
            ext[RIM + i, f] = grid[RIM + i, f].astype(F32)
        for k in range(RIM):
            ext[k, f] = grid[k, f].astype(F32)
            ext[RIM + LATS + k, f] = grid[RIM + LATS + k, f].astype(F32)

    @pl.when(rank[0] == 0)
    def _():
        for f in range(FIELDS):
            for k in range(RIM):
                x = grid[2 * RIM - 1 - k, f].astype(F32)
                ext[k, f] = jnp.concatenate([x[40:], x[:40]], axis=0)

    @pl.when(rank[0] == BANDS * WAVES - 1)
    def _():
        for f in range(FIELDS):
            for k in range(RIM):
                x = grid[RIM + LATS - 1 - k, f].astype(F32)
                up = jnp.concatenate([x[1:], x[:1]], axis=0)
                down = jnp.concatenate([x[79:], x[:79]], axis=0)
                ext[RIM + LATS + k, f] = jnp.where(row_odd, down, up)

    def shift_row(r, _):
        for f in range(FIELDS):
            x = ext[r, f]
            moved[3, r, f] = x
            up = jnp.concatenate([x[2:], x[:2]], axis=0)
            down = jnp.concatenate([x[78:], x[:78]], axis=0)
            both = jnp.concatenate([x, up, down], axis=1).astype(BF16)
            ahead = jnp.dot(both[:, 0:256], shifts[...], preferred_element_type=F32)
            behind = jnp.dot(
                jnp.concatenate([both[:, 0:128], both[:, 256:384]], axis=1),
                shifts2[...],
                preferred_element_type=F32,
            )
            for c in range(3):
                moved[4 + c, r, f] = ahead[:, 128 * c : 128 * c + 128]
                moved[c, r, f] = behind[:, 128 * c : 128 * c + 128]
        return 0

    rowi = lax.broadcasted_iota(jnp.int32, (256, 384), 0)
    coli = lax.broadcasted_iota(jnp.int32, (256, 384), 1)
    by = coli // 128 + 1
    want = (coli & 127) + by
    shifts[...] = jnp.where(rowi == want, 1.0, 0.0).astype(BF16)
    by = coli // 128 - 3
    want = (coli & 127) + by
    want = jnp.where(want < 0, want + 256, want)
    shifts2[...] = jnp.where(rowi == want, 1.0, 0.0).astype(BF16)
    lax.fori_loop(0, LATS + 2 * RIM, shift_row, 0, unroll=11)

    def chunk(n, _):
        i, start = n // 10, pl.multiple_of(lax.rem(n, 10) * 8, 8)
        at = pl.multiple_of(n * 8, 8)
        e = code[pl.ds(at, 8), :]
        t = pick[pl.ds(at, 8), :]
        taps = [
            jnp.take_along_axis(jnp.broadcast_to(taps_of[k : k + 1, :], (8, 128)), t, axis=1)
            for k in range(16)
        ]
        x0, x1 = (e & 1) == 1, (e & 2) == 2
        y0, y1 = (e & 4) == 4, (e & 8) == 8
        columns = [spread([taps[4 * a + b] for a in range(4)], y0, 1) for b in range(4)]
        columns = [spread(column, y1, 2) for column in columns]
        total = [jnp.zeros((8, 128), F32) for _ in range(FIELDS)]
        for sr in range(7):
            factors = spread(spread([columns[b][sr] for b in range(4)], x0, 1), x1, 2)
            for sc in range(7):
                for f in range(FIELDS):
                    total[f] = total[f] + factors[sc] * moved[sc, i + sr, f, pl.ds(start, 8), :]
        for f in range(FIELDS):
            summed[i, f, pl.ds(start, 8), :] = total[f]
        return 0

    lax.fori_loop(0, 50, chunk, 0, unroll=10)
    for n in range(LATS * FIELDS):
        i, f = n // FIELDS, n % FIELDS
        value = summed[i, f].astype(BF16)
        arrival[f, 80 * i : 80 * i + 80, :] = value
        both = jnp.dot(dft_back[...], value, preferred_element_type=F32)
        mixed[80 * n : 80 * n + 80, :] = both[0:80]
        mixed[1600 + 80 * n : 1680 + 80 * n, :] = both[80:160]
    by_pair[...] = jnp.zeros((640, 512), BF16)
    for m1 in range(M1):
        right = jnp.concatenate(
            [mixed[pl.ds(m1, 40, stride=M1), :], mixed[pl.ds(1600 + m1, 40, stride=M1), :]], axis=1
        ).astype(BF16)
        part = lax.dot_general(phase[64 * m1 : 64 * m1 + 64, :], right, NT, preferred_element_type=F32)
        part = (part * scale).astype(BF16)
        low, high = pl.ds(P2 * m1, P2), pl.ds(P2 * (M1 - 1 - m1), P2)
        for k, where in enumerate((low, low, high, high)):
            by_pair[where, 128 * k : 128 * k + 40] = part[16 * k : 16 * k + 16]
    ordered = jnp.dot(by_pair[...], sel_back[...], preferred_element_type=F32).astype(BF16)
    row = lax.broadcasted_iota(jnp.int32, (640, 640), 0)
    onehot = jnp.where(row == order_of(place[...].reshape(1, 640)), 1.0, 0.0).astype(BF16)
    slots = lax.dot_general(onehot, ordered, TN, preferred_element_type=F32)
    back[...] = jnp.concatenate(
        [slots[:, 0:128].reshape(80, 8, 128), slots[:, 128:256].reshape(80, 8, 128)], axis=1
    ).astype(BF16).reshape(WAVES, GROUPS, 16, 128)


def stencil(rank, grid, code, pick, weight, quad, place, phase, dft_back, sel_back):
    smem = pl.BlockSpec(memory_space=pltpu.SMEM)
    return pl.pallas_call(
        stencil_kernel,
        out_shape=(
            jax.ShapeDtypeStruct((FIELDS, 2 * LATS * Q1, Q2), BF16),
            jax.ShapeDtypeStruct((WAVES, GROUPS, 16, 128), BF16),
        ),
        in_specs=[smem] + whole(4) + [smem] + whole(4),
        out_specs=tuple(whole(2)),
        scratch_shapes=[
            pltpu.VMEM((LATS + 2 * RIM, FIELDS, 80, Q2), F32),
            pltpu.VMEM((7, LATS + 2 * RIM, FIELDS, 80, Q2), F32),
            pltpu.VMEM((LATS, FIELDS, 80, Q2), F32),
            pltpu.VMEM((3200, 128), F32),
            pltpu.VMEM((640, 512), BF16),
            pltpu.VMEM((16, 128), F32),
            pltpu.VMEM((256, 384), BF16),
            pltpu.VMEM((256, 384), BF16),
        ],
        compiler_params=pltpu.CompilerParams(vmem_limit_bytes=VMEM_LIMIT),
    )(rank, grid, code, pick, weight, quad, place, phase, dft_back, sel_back)


def grid_view(x):
    return x.reshape(2, LATS, Q1, Q2).transpose(1, 2, 0, 3).reshape(2 * LATS * Q1, Q2)


def per_device(
    spectral, legendre, slot_pair, quad_weight, depart_code, stencil_pick, stencil_weight
):
    phase, dft, dft_back, sel, sel_back = [jnp.asarray(t) for t in phase_tables()]
    wave_rank = lax.axis_index("wave")
    band_rank = lax.axis_index("band")
    pairs = slot_pair
    rank = (band_rank * WAVES + wave_rank).reshape(1)
    own = spectral.transpose(0, 2, 1).reshape(8 * SLOTS, ROWS)
    four = forward(pairs, own, legendre)
    grid = to_grid(slot_pair, four, phase, dft, sel)
    arrival, back = stencil(
        rank, grid, grid_view(depart_code), grid_view(stencil_pick), stencil_weight, quad_weight,
        slot_pair, phase, dft_back, sel_back,
    )
    total = backward(pairs, back, legendre)
    spectral_out = total.reshape(SLOTS, 8, 128)[:, :, :ROWS].transpose(0, 2, 1)
    arrival = arrival.reshape(FIELDS, LATS, Q1, 2, Q2).transpose(0, 3, 1, 2, 4)
    return arrival.reshape(1, FIELDS, 2, LATS, NLON), spectral_out


def solution(mesh):
    lat = ("band", "wave")
    in_specs = (
        P("wave", "band", None),
        P("wave", "band", None),
        P(),
        P("band"),
        P(None, None, lat, None),
        P(None, None, lat, None),
        P(),
    )
    out_specs = (P(None, None, None, lat, None), P("wave", "band", None))
    return jax.shard_map(
        per_device, mesh=mesh, in_specs=in_specs, out_specs=out_specs, check_vma=False
    )
```

```python
import functools
import math

import jax
import jax.numpy as jnp
import numpy as np
from jax import lax
from jax.experimental import pallas as pl
from jax.experimental.pallas import tpu as pltpu
from jax.sharding import PartitionSpec as P

M = 1280
NLON = 5120
FIELDS = 4
WAVES = 16
BANDS = 16
SLOTS = 40
ROWS = 88
NROW = ROWS * BANDS
LATS = 5
BAND_LATS = LATS * WAVES
Q1 = 40
Q2 = 128
M1 = 40
P2 = 16
LANES = 256
RIM = 3
MESH = pl.DeviceIdType.MESH
F32 = jnp.float32
BF16 = jnp.bfloat16
VMEM_LIMIT = 50 * 1024 * 1024
NT = (((1,), (1,)), ((), ()))
TN = (((0,), (0,)), ((), ()))


def phase_tables():
    m1 = np.arange(M1)[:, None, None]
    p2 = np.arange(P2)[None, :, None]
    q2 = np.arange(Q2)[None, None, :]
    e = np.zeros((M1, 2, 2, P2, 2, Q2))
    for o, m in enumerate((m1 + M1 * p2, m1 + M1 * (31 - p2))):
        a = 2 * np.pi * ((m * q2) % NLON) / NLON
        e[:, o, 0, :, 0] = np.cos(a)
        e[:, o, 0, :, 1] = np.sin(a)
        e[:, o, 1, :, 0] = -np.sin(a)
        e[:, o, 1, :, 1] = np.cos(a)
    a = 2 * np.pi * (np.outer(np.arange(Q1), np.arange(M1)) % M1) / M1
    t = np.zeros((Q1, 2, 2, 2, M1))
    for h in range(2):
        t[:, h, 0, h] = np.cos(a)
        t[:, h, 1, h] = -np.sin(a)
    t = t.reshape(Q1 * 2, 4 * M1)
    sel = np.zeros((LANES, 4, 128))
    for i in range(LATS):
        for o in range(2):
            for h in range(2):
                for f in range(FIELDS):
                    for r in range(2):
                        lane = i * 32 + ((o * 2 + h) * FIELDS + f) * 2 + r
                        sel[lane, o * 2 + r, (i * FIELDS + f) * 2 + h] = 1
    sel = sel.reshape(LANES, 512)
    return [
        v.astype(np.float32).astype(jnp.bfloat16)
        for v in (e.reshape(M1 * 64, 256), t, t.T.copy(), sel, sel.T.copy())
    ]


GROUPS = 5
GROUP = SLOTS // GROUPS
TALL = 8 * GROUP
HALF = TALL // 2
WIDE = 384
STEPS = (1, 3, 2)
SIDE = 4


def row_marks(pair, shape):
    j = lax.broadcasted_iota(jnp.int32, shape, 1)
    low_count = M - pair
    higher = j >= low_count
    degree = jnp.where(higher, j - low_count, j)
    sign = (1 - 2 * (degree & 1)).astype(F32)
    return higher, jnp.where(j <= M, 1.0, 0.0), sign


class Plane:
    def __init__(self, k):
        band = lax.axis_index("band")
        x, y = band // SIDE, lax.rem(band, SIDE)
        self.x_first = k == 0
        self.u, self.v = (x, y) if self.x_first else (y, x)

    def along_u(self, by):
        u = turn(self.u, by)
        return {"band": u * SIDE + self.v if self.x_first else self.v * SIDE + u}

    def along_v(self, by):
        v = turn(self.v, by)
        return {"band": self.u * SIDE + v if self.x_first else v * SIDE + self.u}


def side_by_side(pieces):
    return jnp.concatenate(pieces + [jnp.zeros((8, WIDE - 4 * ROWS), F32)], axis=1).astype(BF16)


def turn(at, by):
    return lax.rem(at + by, SIDE)


def greet():
    barrier = pltpu.get_barrier_semaphore()
    me = lax.axis_index("wave")
    plane = Plane(0)
    for by in (1, 3, 2):
        for where in (plane.along_u(by), plane.along_v(by)):
            pl.semaphore_signal(barrier, inc=1, device_id=where, device_id_type=MESH)
    for d in range(1, WAVES):
        pl.semaphore_signal(
            barrier, inc=1, device_id={"wave": lax.rem(me + d, WAVES)}, device_id_type=MESH
        )
    return barrier, 6 + WAVES - 1


def remote(src, dst, send_sem, recv_sem, where):
    return pltpu.make_async_remote_copy(
        src_ref=src, dst_ref=dst, send_sem=send_sem, recv_sem=recv_sem,
        device_id=where, device_id_type=MESH,
    )


def wave_copies(src, dst, g, send_sem, recv_sem):
    me = lax.axis_index("wave")
    copies = []
    for d in sorted(range(1, WAVES), key=lambda d: (abs(d - WAVES // 2), d)):
        peer = lax.rem(me + d, WAVES)
        copies.append(
            remote(src.at[peer, g], dst.at[me, g], send_sem.at[g, d], recv_sem.at[g, d], {"wave": peer})
        )
    return copies


def forward_kernel(
    pairs, spec_hbm, leg_hbm, out,
    spec, leg, gath, rows, held, packed, leg_sem, spec_sem, plane_send, plane_recv, wave_send, wave_recv,
):
    me = lax.axis_index("wave")
    spec_load = pltpu.make_async_copy(spec_hbm, spec, spec_sem)
    spec_load.start()
    barrier, greeted = greet()
    spec_load.wait()
    loads = [
        pltpu.make_async_copy(
            leg_hbm.at[pl.ds(GROUP * g, GROUP)], leg.at[pl.ds(GROUP * g, GROUP)], leg_sem.at[g]
        )
        for g in range(GROUPS)
    ]
    near, far = [], []
    for g in range(GROUPS):
        for k in range(2):
            p = Plane(k)
            start = TALL * g + HALF * k
            own = spec[start : start + HALF, :].astype(F32)
            own = side_by_side([own[8 * m : 8 * m + 8] for m in range(4)])
            if k == 0:
                gath[g, 0, p.u, p.v] = own
                one, line = gath.at[g, 0, p.u, p.v], gath.at[g, 0, :, p.v]
            else:
                gath[g, 1, p.v, p.u] = own
                one, line = gath.at[g, 1, p.v, p.u], gath.at[g, 1, p.v]
            for n, by in enumerate(STEPS):
                near.append(
                    remote(one, one, plane_send.at[g, k, n], plane_recv.at[g, k, n], p.along_u(by))
                )
                far.append(
                    remote(
                        line, line, plane_send.at[g, k, 3 + n], plane_recv.at[g, k, 3 + n], p.along_v(by)
                    )
                )
    pl.semaphore_wait(barrier, greeted)
    for hop in near:
        hop.start()
    for load in loads:
        load.start()

    sent = []

    def multiply(g):
        for b in range(BANDS):
            for k in range(2):
                block = gath[g, k, b // SIDE, b % SIDE].astype(F32)
                for m in range(4):
                    at = HALF * k + 8 * m
                    rows[at : at + 8, ROWS * b : ROWS * (b + 1)] = block[:, ROWS * m : ROWS * (m + 1)]

        def slots(part, _):
            for k in range(4):
                at = part * 4 + k
                s = GROUP * g + at
                pair = pairs[me * SLOTS + s]
                value = rows[pl.ds(pl.multiple_of(8 * at, 8), 8), :]
                higher, used, sign = row_marks(pair, (8, NROW))
                value = value * used
                low = jnp.where(higher, 0.0, value) * jnp.where(pair == 0, 1.0, 2.0)
                high = jnp.where(higher, value, 0.0) * 2.0
                x = jnp.concatenate([low, low * sign, high, high * sign], axis=0).astype(BF16)
                held[pl.ds(pl.multiple_of(BAND_LATS * at, 16), BAND_LATS), 0:32] = lax.dot_general(
                    leg[s], x, NT, preferred_element_type=F32
                )
            return 0

        lax.fori_loop(0, GROUP // 4, slots, 0, unroll=2)
        for w in range(WAVES):
            part = [held[pl.ds(LATS * w + i, GROUP, stride=BAND_LATS), :][:, 0:32] for i in range(LATS)]
            first = jnp.concatenate(part[:4], axis=1)
            second = jnp.concatenate([part[4], jnp.zeros((GROUP, 96), F32)], axis=1)
            packed[w, g] = jnp.concatenate([first, second], axis=0).astype(BF16)
        copies = wave_copies(packed, out, g, wave_send, wave_recv)
        for copy in copies:
            copy.start()
        out[me, g] = packed[me, g]
        sent.extend(copies)

    for g in range(GROUPS):
        for k in range(6):
            near[6 * g + k].wait_recv()
        for k in range(6):
            far[6 * g + k].start()
    for g in range(GROUPS):
        for k in range(6):
            far[6 * g + k].wait_recv()
        loads[g].wait()
        multiply(g)
    for hop in near + far:
        hop.wait_send()
    for copy in sent:
        copy.wait()


def forward(pairs, spec, leg):
    return pl.pallas_call(
        forward_kernel,
        out_shape=jax.ShapeDtypeStruct((WAVES, GROUPS, 16, 128), BF16),
        in_specs=[
            pl.BlockSpec(memory_space=pltpu.SMEM),
            pl.BlockSpec(memory_space=pl.ANY),
            pl.BlockSpec(memory_space=pl.ANY),
        ],
        out_specs=pl.BlockSpec(memory_space=pltpu.VMEM),
        scratch_shapes=[
            pltpu.VMEM((8 * SLOTS, ROWS), BF16),
            pltpu.VMEM((SLOTS, BAND_LATS, NROW), BF16),
            pltpu.VMEM((GROUPS, 2, SIDE, SIDE, 8, WIDE), BF16),
            pltpu.VMEM((TALL, NROW), F32),
            pltpu.VMEM((GROUP * BAND_LATS, 128), F32),
            pltpu.VMEM((WAVES, GROUPS, 16, 128), BF16),
            pltpu.SemaphoreType.DMA((GROUPS,)),
            pltpu.SemaphoreType.DMA,
            pltpu.SemaphoreType.DMA((GROUPS, 2, 6)),
            pltpu.SemaphoreType.DMA((GROUPS, 2, 6)),
            pltpu.SemaphoreType.DMA((GROUPS, WAVES)),
            pltpu.SemaphoreType.DMA((GROUPS, WAVES)),
        ],
        compiler_params=pltpu.CompilerParams(
            collective_id=1, has_side_effects=True, vmem_limit_bytes=VMEM_LIMIT
        ),
    )(pairs, spec, leg)


def backward_kernel(
    pairs, coef, leg_hbm, out,
    leg, recv, held, tall, part, first, line, line_out, second,
    leg_sem, wave_send, wave_recv, plane_send, plane_recv,
):
    me = lax.axis_index("wave")
    barrier, greeted = greet()
    loads = [
        pltpu.make_async_copy(
            leg_hbm.at[pl.ds(GROUP * g, GROUP)], leg.at[pl.ds(GROUP * g, GROUP)], leg_sem.at[g]
        )
        for g in range(GROUPS)
    ]
    for load in loads:
        load.start()
    near, far = [], []
    for g in range(GROUPS):
        for k in range(2):
            p = Plane(k)
            for n, by in enumerate(STEPS):
                u, v = turn(p.u, by), turn(p.v, by)
                src = part.at[g, 0, u] if k == 0 else part.at[g, 1, :, u]
                near.append(
                    remote(
                        src, first.at[g, k, n], plane_send.at[g, k, n], plane_recv.at[g, k, n], p.along_u(by)
                    )
                )
                far.append(
                    remote(
                        line_out.at[g, k, v], second.at[g, k, n],
                        plane_send.at[g, k, 3 + n], plane_recv.at[g, k, 3 + n], p.along_v(by),
                    )
                )
    pl.semaphore_wait(barrier, greeted)
    waves = [wave_copies(coef, recv, g, wave_send, wave_recv) for g in range(GROUPS)]
    for copies in waves:
        for copy in copies:
            copy.start()
    recv[me] = coef[me]

    def multiply(g):
        for w in range(WAVES):
            block = recv[w, g].astype(F32)
            for i in range(LATS):
                value = block[8:16] if i == 4 else block[0:8]
                if 0 < i < 4:
                    value = pltpu.roll(value, 128 - 32 * i, 1)
                held[pl.ds(LATS * w + i, GROUP, stride=BAND_LATS), :] = value

        def slots(piece, _):
            for k in range(4):
                at = piece * 4 + k
                s = GROUP * g + at
                lats = held[pl.ds(pl.multiple_of(BAND_LATS * at, 16), BAND_LATS), :][:, 0:32]
                both = lax.dot_general(lats.astype(BF16), leg[s], TN, preferred_element_type=F32)
                higher, used, sign = row_marks(pairs[me * SLOTS + s], (8, NROW))
                low = both[0:8] + sign * both[8:16]
                high = both[16:24] + sign * both[24:32]
                tall[pl.ds(pl.multiple_of(8 * at, 8), 8), :] = jnp.where(higher, high, low) * used
            return 0

        lax.fori_loop(0, GROUP // 4, slots, 0, unroll=2)
        for b in range(BANDS):
            for k in range(2):
                part[g, k, b // SIDE, b % SIDE] = side_by_side(
                    [
                        tall[HALF * k + 8 * m : HALF * k + 8 * m + 8, ROWS * b : ROWS * (b + 1)]
                        for m in range(4)
                    ]
                )

    for g in range(GROUPS):
        for copy in waves[g]:
            copy.wait_recv()
        loads[g].wait()
        multiply(g)
        for k in range(6):
            near[6 * g + k].start()
    for g in range(GROUPS):
        for k in range(2):
            p = Plane(k)
            total = (part[g, 0, p.u] if k == 0 else part[g, 1, :, p.u]).astype(F32)
            for n in range(3):
                near[6 * g + 3 * k + n].wait_recv()
                total = total + first[g, k, n].astype(F32)
            line[g, k] = total
            line_out[g, k] = total.astype(BF16)
            for n in range(3):
                far[6 * g + 3 * k + n].start()
    for g in range(GROUPS):
        for k in range(2):
            total = line[g, k, Plane(k).v]
            for n in range(3):
                far[6 * g + 3 * k + n].wait_recv()
                total = total + second[g, k, n].astype(F32)
            start = TALL * g + HALF * k
            pieces = [
                jnp.concatenate(
                    [total[:, ROWS * m : ROWS * (m + 1)], jnp.zeros((8, 128 - ROWS), F32)], axis=1
                )
                for m in range(4)
            ]
            out[start : start + HALF, :] = jnp.concatenate(pieces, axis=0).astype(BF16)
    for hop in near + far:
        hop.wait_send()
    for copies in waves:
        for copy in copies:
            copy.wait_send()


def backward(pairs, coef, leg):
    return pl.pallas_call(
        backward_kernel,
        out_shape=jax.ShapeDtypeStruct((8 * SLOTS, 128), BF16),
        in_specs=[
            pl.BlockSpec(memory_space=pltpu.SMEM),
            pl.BlockSpec(memory_space=pltpu.VMEM),
            pl.BlockSpec(memory_space=pl.ANY),
        ],
        out_specs=pl.BlockSpec(memory_space=pltpu.VMEM),
        scratch_shapes=[
            pltpu.VMEM((SLOTS, BAND_LATS, NROW), BF16),
            pltpu.VMEM((WAVES, GROUPS, 16, 128), BF16),
            pltpu.VMEM((GROUP * BAND_LATS, 128), F32),
            pltpu.VMEM((TALL, NROW), F32),
            pltpu.VMEM((GROUPS, 2, SIDE, SIDE, 8, WIDE), BF16),
            pltpu.VMEM((GROUPS, 2, 3, SIDE, 8, WIDE), BF16),
            pltpu.VMEM((GROUPS, 2, SIDE, 8, WIDE), F32),
            pltpu.VMEM((GROUPS, 2, SIDE, 8, WIDE), BF16),
            pltpu.VMEM((GROUPS, 2, 3, 8, WIDE), BF16),
            pltpu.SemaphoreType.DMA((GROUPS,)),
            pltpu.SemaphoreType.DMA((GROUPS, WAVES)),
            pltpu.SemaphoreType.DMA((GROUPS, WAVES)),
            pltpu.SemaphoreType.DMA((GROUPS, 2, 6)),
            pltpu.SemaphoreType.DMA((GROUPS, 2, 6)),
        ],
        compiler_params=pltpu.CompilerParams(
            collective_id=2, has_side_effects=True, vmem_limit_bytes=VMEM_LIMIT
        ),
    )(pairs, coef, leg)


def to_grid_kernel(place, four, phase, dft, sel, grid, by_pair, mixed, send_sem, recv_sem):
    rank = lax.axis_index("band") * WAVES + lax.axis_index("wave")
    total = BANDS * WAVES
    ends = (lax.rem(rank + 1, total), lax.rem(rank + total - 1, total))
    ids = [{"band": r // WAVES, "wave": lax.rem(r, WAVES)} for r in ends]
    barrier = pltpu.get_barrier_semaphore()
    for where in ids:
        pl.semaphore_signal(barrier, inc=1, device_id=where, device_id_type=MESH)
    row = lax.broadcasted_iota(jnp.int32, (640, 640), 0)
    onehot = jnp.where(row == order_of(place[...].reshape(1, 640)), 1.0, 0.0).astype(BF16)
    blocks = four[...].astype(F32)
    slots = jnp.concatenate(
        [blocks[:, :, 0:8].reshape(640, 128), blocks[:, :, 8:16].reshape(640, 128)], axis=1
    ).astype(BF16)
    ordered = jnp.dot(onehot, slots, preferred_element_type=F32).astype(BF16)
    by_pair[...] = jnp.dot(ordered, sel[...], preferred_element_type=F32).astype(BF16)
    for m1 in range(M1):
        low, high = pl.ds(P2 * m1, P2), pl.ds(P2 * (M1 - 1 - m1), P2)
        left = jnp.concatenate(
            [by_pair[low, 0:128], by_pair[low, 128:256], by_pair[high, 256:384], by_pair[high, 384:512]],
            axis=0,
        )
        part = lax.dot_general(left, phase[64 * m1 : 64 * m1 + 64, :], TN, preferred_element_type=F32)
        mixed[pl.ds(m1, 40, stride=M1), :] = part[0:40, 0:128]
        mixed[pl.ds(1600 + m1, 40, stride=M1), :] = part[0:40, 128:256]
    for n in range(LATS * FIELDS):
        right = jnp.concatenate(
            [mixed[80 * n : 80 * n + 80, :], mixed[1600 + 80 * n : 1680 + 80 * n, :]], axis=0
        ).astype(BF16)
        grid[RIM + n // FIELDS, n % FIELDS] = jnp.dot(
            dft[...], right, preferred_element_type=F32
        ).astype(BF16)
    pl.semaphore_wait(barrier, 2)
    copies = [
        remote(grid.at[pl.ds(a, RIM)], grid.at[pl.ds(b, RIM)], send_sem.at[k], recv_sem.at[k], ids[k])
        for k, (a, b) in enumerate(((LATS, 0), (RIM, RIM + LATS)))
    ]
    for copy in copies:
        copy.start()
    for copy in copies:
        copy.wait()


def order_of(pair):
    p2 = (pair * 1639) >> 16
    return (pair - M1 * p2) * P2 + p2


def whole(n):
    return [pl.BlockSpec(memory_space=pltpu.VMEM)] * n


def to_grid(place, four, phase, dft, sel):
    return pl.pallas_call(
        to_grid_kernel,
        out_shape=jax.ShapeDtypeStruct((LATS + 2 * RIM, FIELDS, 80, Q2), BF16),
        in_specs=whole(5),
        out_specs=whole(1)[0],
        scratch_shapes=[
            pltpu.VMEM((640, 512), BF16),
            pltpu.VMEM((3200, 128), F32),
            pltpu.SemaphoreType.DMA((2,)),
            pltpu.SemaphoreType.DMA((2,)),
        ],
        compiler_params=pltpu.CompilerParams(
            collective_id=3, has_side_effects=True, vmem_limit_bytes=VMEM_LIMIT
        ),
    )(place, four, phase, dft, sel)


def spread(values, bit, step):
    n = len(values)
    out = []
    for k in range(n + step):
        keep = values[k] if k < n else 0.0
        moved = values[k - step] if k >= step else 0.0
        out.append(jnp.where(bit, moved, keep))
    return out


def stencil_kernel(
    rank, grid, code, pick, weight, quad, place, phase, dft_back, sel_back,
    arrival, back, ext, moved, summed, mixed, by_pair, taps_of, shifts, shifts2,
):
    wave = lax.axis_index("wave")
    lat = lax.broadcasted_iota(jnp.int32, (1, 40), 1) // (2 * FIELDS)
    scale = jnp.zeros((1, 40), F32)
    for i in range(LATS):
        scale = jnp.where(lat == i, quad[wave * LATS + i] / math.sqrt(NLON), scale)
    wide = jnp.concatenate([weight[...], jnp.zeros((16, 112), F32)], axis=1)
    taps_of[...] = jnp.concatenate([wide, jnp.zeros((112, 128), F32)], axis=0).T[0:16]
    row_odd = (lax.broadcasted_iota(jnp.int32, (80, Q2), 0) & 1) == 1
    for f in range(FIELDS):
        for i in range(LATS):
            ext[RIM + i, f] = grid[RIM + i, f].astype(F32)
        for k in range(RIM):
            ext[k, f] = grid[k, f].astype(F32)
            ext[RIM + LATS + k, f] = grid[RIM + LATS + k, f].astype(F32)

    @pl.when(rank[0] == 0)
    def _():
        for f in range(FIELDS):
            for k in range(RIM):
                x = grid[2 * RIM - 1 - k, f].astype(F32)
                ext[k, f] = jnp.concatenate([x[40:], x[:40]], axis=0)

    @pl.when(rank[0] == BANDS * WAVES - 1)
    def _():
        for f in range(FIELDS):
            for k in range(RIM):
                x = grid[RIM + LATS - 1 - k, f].astype(F32)
                up = jnp.concatenate([x[1:], x[:1]], axis=0)
                down = jnp.concatenate([x[79:], x[:79]], axis=0)
                ext[RIM + LATS + k, f] = jnp.where(row_odd, down, up)

    def shift_row(r, _):
        for f in range(FIELDS):
            x = ext[r, f]
            moved[3, r, f] = x
            up = jnp.concatenate([x[2:], x[:2]], axis=0)
            down = jnp.concatenate([x[78:], x[:78]], axis=0)
            both = jnp.concatenate([x, up, down], axis=1).astype(BF16)
            ahead = jnp.dot(both[:, 0:256], shifts[...], preferred_element_type=F32)
            behind = jnp.dot(
                jnp.concatenate([both[:, 0:128], both[:, 256:384]], axis=1),
                shifts2[...],
                preferred_element_type=F32,
            )
            for c in range(3):
                moved[4 + c, r, f] = ahead[:, 128 * c : 128 * c + 128]
                moved[c, r, f] = behind[:, 128 * c : 128 * c + 128]
        return 0

    rowi = lax.broadcasted_iota(jnp.int32, (256, 384), 0)
    coli = lax.broadcasted_iota(jnp.int32, (256, 384), 1)
    by = coli // 128 + 1
    want = (coli & 127) + by
    shifts[...] = jnp.where(rowi == want, 1.0, 0.0).astype(BF16)
    by = coli // 128 - 3
    want = (coli & 127) + by
    want = jnp.where(want < 0, want + 256, want)
    shifts2[...] = jnp.where(rowi == want, 1.0, 0.0).astype(BF16)
    lax.fori_loop(0, LATS + 2 * RIM, shift_row, 0, unroll=11)

    def chunk(n, _):
        i, start = n // 10, pl.multiple_of(lax.rem(n, 10) * 8, 8)
        at = pl.multiple_of(n * 8, 8)
        e = code[pl.ds(at, 8), :]
        t = pick[pl.ds(at, 8), :]
        taps = [
            jnp.take_along_axis(jnp.broadcast_to(taps_of[k : k + 1, :], (8, 128)), t, axis=1)
            for k in range(16)
        ]
        x0, x1 = (e & 1) == 1, (e & 2) == 2
        y0, y1 = (e & 4) == 4, (e & 8) == 8
        columns = [spread([taps[4 * a + b] for a in range(4)], y0, 1) for b in range(4)]
        columns = [spread(column, y1, 2) for column in columns]
        total = [jnp.zeros((8, 128), F32) for _ in range(FIELDS)]
        for sr in range(7):
            factors = spread(spread([columns[b][sr] for b in range(4)], x0, 1), x1, 2)
            for sc in range(7):
                for f in range(FIELDS):
                    total[f] = total[f] + factors[sc] * moved[sc, i + sr, f, pl.ds(start, 8), :]
        for f in range(FIELDS):
            summed[i, f, pl.ds(start, 8), :] = total[f]
        return 0

    lax.fori_loop(0, 50, chunk, 0, unroll=10)
    for n in range(LATS * FIELDS):
        i, f = n // FIELDS, n % FIELDS
        value = summed[i, f].astype(BF16)
        arrival[f, 80 * i : 80 * i + 80, :] = value
        both = jnp.dot(dft_back[...], value, preferred_element_type=F32)
        mixed[80 * n : 80 * n + 80, :] = both[0:80]
        mixed[1600 + 80 * n : 1680 + 80 * n, :] = both[80:160]
    by_pair[...] = jnp.zeros((640, 512), BF16)
    for m1 in range(M1):
        right = jnp.concatenate(
            [mixed[pl.ds(m1, 40, stride=M1), :], mixed[pl.ds(1600 + m1, 40, stride=M1), :]], axis=1
        ).astype(BF16)
        part = lax.dot_general(phase[64 * m1 : 64 * m1 + 64, :], right, NT, preferred_element_type=F32)
        part = (part * scale).astype(BF16)
        low, high = pl.ds(P2 * m1, P2), pl.ds(P2 * (M1 - 1 - m1), P2)
        for k, where in enumerate((low, low, high, high)):
            by_pair[where, 128 * k : 128 * k + 40] = part[16 * k : 16 * k + 16]
    ordered = jnp.dot(by_pair[...], sel_back[...], preferred_element_type=F32).astype(BF16)
    row = lax.broadcasted_iota(jnp.int32, (640, 640), 0)
    onehot = jnp.where(row == order_of(place[...].reshape(1, 640)), 1.0, 0.0).astype(BF16)
    slots = lax.dot_general(onehot, ordered, TN, preferred_element_type=F32)
    back[...] = jnp.concatenate(
        [slots[:, 0:128].reshape(80, 8, 128), slots[:, 128:256].reshape(80, 8, 128)], axis=1
    ).astype(BF16).reshape(WAVES, GROUPS, 16, 128)


def stencil(rank, grid, code, pick, weight, quad, place, phase, dft_back, sel_back):
    smem = pl.BlockSpec(memory_space=pltpu.SMEM)
    return pl.pallas_call(
        stencil_kernel,
        out_shape=(
            jax.ShapeDtypeStruct((FIELDS, 2 * LATS * Q1, Q2), BF16),
            jax.ShapeDtypeStruct((WAVES, GROUPS, 16, 128), BF16),
        ),
        in_specs=[smem] + whole(4) + [smem] + whole(4),
        out_specs=tuple(whole(2)),
        scratch_shapes=[
            pltpu.VMEM((LATS + 2 * RIM, FIELDS, 80, Q2), F32),
            pltpu.VMEM((7, LATS + 2 * RIM, FIELDS, 80, Q2), F32),
            pltpu.VMEM((LATS, FIELDS, 80, Q2), F32),
            pltpu.VMEM((3200, 128), F32),
            pltpu.VMEM((640, 512), BF16),
            pltpu.VMEM((16, 128), F32),
            pltpu.VMEM((256, 384), BF16),
            pltpu.VMEM((256, 384), BF16),
        ],
        compiler_params=pltpu.CompilerParams(vmem_limit_bytes=VMEM_LIMIT),
    )(rank, grid, code, pick, weight, quad, place, phase, dft_back, sel_back)


def grid_view(x):
    return x.reshape(2, LATS, Q1, Q2).transpose(1, 2, 0, 3).reshape(2 * LATS * Q1, Q2)


def per_device(
    spectral, legendre, slot_pair, quad_weight, depart_code, stencil_pick, stencil_weight
):
    phase, dft, dft_back, sel, sel_back = [jnp.asarray(t) for t in phase_tables()]
    wave_rank = lax.axis_index("wave")
    band_rank = lax.axis_index("band")
    pairs = slot_pair
    rank = (band_rank * WAVES + wave_rank).reshape(1)
    own = spectral.transpose(0, 2, 1).reshape(8 * SLOTS, ROWS)
    four = forward(pairs, own, legendre)
    grid = to_grid(slot_pair, four, phase, dft, sel)
    arrival, back = stencil(
        rank, grid, grid_view(depart_code), grid_view(stencil_pick), stencil_weight, quad_weight,
        slot_pair, phase, dft_back, sel_back,
    )
    total = backward(pairs, back, legendre)
    spectral_out = total.reshape(SLOTS, 8, 128)[:, :, :ROWS].transpose(0, 2, 1)
    arrival = arrival.reshape(FIELDS, LATS, Q1, 2, Q2).transpose(0, 3, 1, 2, 4)
    return arrival.reshape(1, FIELDS, 2, LATS, NLON), spectral_out


def solution(mesh):
    lat = ("band", "wave")
    in_specs = (
        P("wave", "band", None),
        P("wave", "band", None),
        P(),
        P("band"),
        P(None, None, lat, None),
        P(None, None, lat, None),
        P(),
    )
    out_specs = (P(None, None, None, lat, None), P("wave", "band", None))
    return jax.shard_map(
        per_device, mesh=mesh, in_specs=in_specs, out_specs=out_specs, check_vma=False
    )
```
